32 devices in a mesh: cases: 2 (over y), blk: 8 (over z, x), state: 2 (over core).
Axes of the slice: x: 2, y: 2, z: 4, core: 2. Of those that a mesh axis runs over, the one named last changes fastest.
Arguments:
- base_real: float32 [32768], P(('cases', 'blk', 'state')), parts along dimension 0, may hold values from -6 to 6
- base_reactive: float32 [32768], P(('cases', 'blk', 'state')), parts along dimension 0, may hold values from 0.2 to 1
- voltage: float32 [32768], P(('cases', 'blk', 'state')), parts along dimension 0, may hold values from 0.9 to 1.1
- rating: float32 [32768], P(('cases', 'blk', 'state')), parts along dimension 0, may hold values from 1 to 4
- monitored: int32 [16384], P(('cases', 'blk', 'state')), parts along dimension 0, may hold values from 0 to 2047, as said below
- tile_ids: int32 [128, 4], P(('cases', 'blk', 'state')), parts along dimension 0, may hold values from -1 to 7, as said below
- tile_values: bfloat16 [128, 4, 128, 128], P(('cases', 'blk', 'state')), parts along dimension 0, may hold values from -0.5 to 0.5
- outage_ids: int32 [16, 128], P(('cases', 'blk')), parts along dimension 0, may hold values from 0 to 2047, as said below
- coupling: bfloat16 [16, 128, 128], P(('cases', 'blk')), parts along dimension 0, may hold values from -0.5 to 0.5
- outage_pairs: int32 [16, 2, 128], P(('cases', 'blk')), parts along dimension 0, may hold values from 0 to 127, as said below
Outputs:
- branch_peak: float32 [16384], P(('cases', 'blk', 'state')), parts along dimension 0
- worst_loading: float32 [16, 128], P(('cases', 'blk'), 'state'), parts along dimension 0
The draws below stay inside these ranges and needn't reach their ends.
There are 2 independent parts, one for each index of `cases`. The reference program is written for one: setup_inputs(seed, part) draws one part's arguments, and reference() takes and returns one part's arrays. A program takes and returns all parts, laid end to end along the dimension named above; each array names one. Nothing has to cross between parts.
Inputs may be any that keep to these rules, and one draw needn't show every extreme that they name: `monitored`: the 1024 entries of one cycle position (entry index // 1024) are distinct. `outage_ids`: each row holds 128 distinct indices. `tile_ids`: each row names between 2 and 4 distinct outage blocks in its first slots and holds -1 in the remaining slots; some row is full. `outage_pairs`: the two branches of a pair differ.
All inputs are finite; a program needn't handle non-finite values.
Results may differ from the reference program's by a relative error of at most 0.0019.
Values may be sent and summed in bfloat16 or wider, within the bound.
A program may use at most 64 MiB of HBM per device.

```python
import math
import jax
import jax.numpy as jnp
from jax import lax

TILE = 128
PAIRS = 128
NBLK = 8
KB = 4
BR_POS = 2048
MON_POS = 1024
BRANCHES = 16384
MON = 8192
MON_TILES = 64


def swap_in(order, value, slot):
    where_at = jnp.argmax(order == value)
    displaced = order[slot]
    order = order.at[where_at].set(displaced)
    return order.at[slot].set(value)


def chosen_rows(key, row_count, span, keep):
    keys = jax.random.split(key, row_count)
    orders = jax.vmap(lambda one_key: jax.random.permutation(one_key, span))(keys).astype(jnp.int32)
    picked = jax.random.randint(jax.random.fold_in(key, 5), (), 0, row_count)
    forced = swap_in(swap_in(orders[picked], 0, 0), span - 1, 1)
    orders = orders.at[picked].set(forced)
    return orders[:, :keep]


def draw_monitored(key, part):
    rows_out = chosen_rows(jax.random.fold_in(key, 11), NBLK, BR_POS, MON_POS)
    return rows_out.reshape(MON).astype(jnp.int32)


def draw_outage_ids(key, part):
    return chosen_rows(jax.random.fold_in(key, 23), NBLK, BR_POS, TILE).astype(jnp.int32)


def draw_tile_ids(key, part):
    base_key = jax.random.fold_in(key, 31)
    orders = chosen_rows(base_key, MON_TILES, NBLK, KB)
    counts = jax.random.randint(jax.random.fold_in(base_key, 7), (MON_TILES,), KB // 2, KB + 1)
    full_row = jax.random.randint(jax.random.fold_in(base_key, 9), (), 0, MON_TILES)
    counts = counts.at[full_row].set(KB)
    counts = counts.at[(full_row + 1) % MON_TILES].set(KB // 2)
    slots = jnp.arange(KB, dtype=jnp.int32)[None, :]
    return jnp.where(slots < counts[:, None], orders, -1).astype(jnp.int32)


def draw_outage_pairs(key, part):
    base_key = jax.random.fold_in(key, 37)
    first_idx = jax.random.randint(jax.random.fold_in(base_key, 1), (NBLK, PAIRS), 0, TILE)
    offset = jax.random.randint(jax.random.fold_in(base_key, 2), (NBLK, PAIRS), 1, TILE)
    second_idx = (first_idx + offset) % TILE
    return jnp.stack([first_idx, second_idx], axis=1).astype(jnp.int32)


def block_scale(own_key, shape, shards, least, high):
    loudness = 1.0
    for axis_at, shards_of in shards:
        steps = jax.random.uniform(jax.random.fold_in(jax.random.fold_in(own_key, 6), axis_at), (shards_of,), jnp.float32, least / len(shards), high / len(shards))
        loudness = loudness * jnp.repeat(jnp.exp(steps), shape[axis_at] // shards_of).reshape((-1,) + (1,) * (len(shape) - 1 - axis_at))
    return loudness


def normal_values(own_key, dims, scale, limit, shards=(), kind=jnp.bfloat16):
    values = scale * jax.random.normal(own_key, dims, jnp.float32)
    if shards:
        values = values * block_scale(own_key, dims, shards, -0.22, 0.18)
    return jnp.clip(values, -limit, limit).astype(kind)


def setup_inputs(seed: int = 0, part: int = 0) -> dict:
    arg_keys = jax.random.split(jax.random.key(seed), 11)
    part_splits = jax.random.split(jax.random.fold_in(arg_keys[10], part), 11)
    return {
        "base_real": normal_values(part_splits[0], (BRANCHES,), 1.0, 6.0, ((0, 16),), jnp.float32),
        "base_reactive": jnp.clip(0.2 + 0.8 * jax.random.uniform(part_splits[1], (BRANCHES,), jnp.float32) ** block_scale(part_splits[1], (BRANCHES,), ((0, 16),), -0.2, 0.2), 0.2, 1.0),
        "voltage": jnp.clip(0.9 + 0.20000005 * jax.random.uniform(part_splits[2], (BRANCHES,), jnp.float32) ** block_scale(part_splits[2], (BRANCHES,), ((0, 16),), -0.2, 0.2), 0.9, 1.1),
        "rating": jnp.clip(jnp.exp(math.log(4.0) - 1.3862944 * jax.random.uniform(part_splits[3], (BRANCHES,), jnp.float32) ** block_scale(part_splits[3], (BRANCHES,), ((0, 16),), -0.2, 0.2)), 1.0, 4.0),
        "monitored": draw_monitored(jax.random.fold_in(jax.random.fold_in(arg_keys[10], part), 71), part),
        "tile_ids": draw_tile_ids(jax.random.fold_in(jax.random.fold_in(arg_keys[10], part), 71), part),
        "tile_values": jnp.clip(jax.random.uniform(part_splits[6], (MON_TILES, KB, TILE, TILE), jnp.float32, -0.5, 0.5) * block_scale(part_splits[6], (MON_TILES, KB, TILE, TILE), ((0, 16),), -0.4, 0.0), -0.5, 0.5).astype(jnp.bfloat16),
        "outage_ids": draw_outage_ids(jax.random.fold_in(jax.random.fold_in(arg_keys[10], part), 71), part),
        "coupling": jnp.clip(jax.random.uniform(part_splits[8], (NBLK, TILE, TILE), jnp.float32, -0.5, 0.5) * block_scale(part_splits[8], (NBLK, TILE, TILE), ((0, 8),), -0.4, 0.0), -0.5, 0.5).astype(jnp.bfloat16),
        "outage_pairs": draw_outage_pairs(jax.random.fold_in(jax.random.fold_in(arg_keys[10], part), 71), part),
    }


def reference(base_real, base_reactive, voltage, rating, monitored, tile_ids, tile_values, outage_ids, coupling, outage_pairs):
    position = jnp.arange(MON, dtype=jnp.int32) // MON_POS
    branch_number = (position * BR_POS + monitored).astype(jnp.int32)
    mon_real = base_real[branch_number].reshape(MON_TILES, TILE)
    mon_reactive = base_reactive[branch_number].reshape(MON_TILES, TILE)
    mon_limit = (voltage[branch_number] * rating[branch_number]).reshape(MON_TILES, TILE)
    react_sq = mon_reactive * mon_reactive
    block_base = jnp.arange(NBLK, dtype=jnp.int32)[:, None] * BR_POS
    outage_flow = base_real[(block_base + outage_ids).astype(jnp.int32)].astype(jnp.bfloat16)
    first_idx = outage_pairs[:, 0, :]
    second_idx = outage_pairs[:, 1, :]
    flow_first = jnp.take_along_axis(outage_flow, first_idx, axis=1).astype(jnp.float32)
    flow_second = jnp.take_along_axis(outage_flow, second_idx, axis=1).astype(jnp.float32)
    block_rows = jnp.arange(NBLK, dtype=jnp.int32)[:, None]
    s_first_second = coupling[block_rows, first_idx, second_idx].astype(jnp.float32)
    s_second_first = coupling[block_rows, second_idx, first_idx].astype(jnp.float32)
    determinant = 1.0 - s_first_second * s_second_first
    w_first = (flow_first + s_first_second * flow_second) / determinant
    w_second = (flow_second + s_second_first * flow_first) / determinant
    matches = tile_ids[:, :, None] == jnp.arange(NBLK, dtype=jnp.int32)[None, None, :]
    slot_table = lax.optimization_barrier(jnp.sum(jnp.where(matches, jnp.arange(KB, dtype=jnp.int32)[None, :, None], 0), axis=1)).astype(jnp.int32)
    present = jnp.any(matches, axis=1)
    rows_iota = lax.broadcasted_iota(jnp.int32, (TILE, PAIRS), 0)
    tile_rows = jnp.arange(MON_TILES, dtype=jnp.int32)

    def per_block(block_now):
        pair_first = first_idx[block_now]
        pair_second = second_idx[block_now]
        weights = (jnp.where(rows_iota == pair_first[None, :], w_first[block_now][None, :], 0.0) + jnp.where(rows_iota == pair_second[None, :], w_second[block_now][None, :], 0.0)).astype(jnp.bfloat16)
        chosen = tile_values[tile_rows, slot_table[:, block_now]].astype(jnp.float32)
        delta = jnp.einsum('tmi,ip->tmp', chosen, weights.astype(jnp.float32), precision=lax.Precision.HIGHEST)
        delta = jnp.where(present[:, block_now][:, None, None], delta, 0.0)
        post = mon_real[:, :, None] + delta
        loading = jnp.sqrt(post * post + react_sq[:, :, None]) / mon_limit[:, :, None]
        return (lax.optimization_barrier(jnp.max(loading, axis=2)), lax.optimization_barrier(jnp.max(loading, axis=(0, 1))))
    peaks, worsts = lax.map(per_block, jnp.arange(NBLK, dtype=jnp.int32))
    branch_peak = lax.optimization_barrier(jnp.max(peaks, axis=0)).reshape(MON)
    return (branch_peak, worsts)
```

```python
import functools

import jax
import jax.numpy as jnp
from jax import lax
from jax.experimental import pallas as pl
from jax.experimental.pallas import tpu as pltpu
from jax.sharding import PartitionSpec as P

MESH = pl.DeviceIdType.MESH
LANES = 128


def take_lanes(row, lanes):
    spread = jnp.broadcast_to(row, lanes.shape)
    return jnp.take_along_axis(spread, lanes, axis=1, mode="promise_in_bounds")


def lookup(table, high, low, first_row):
    found = jnp.zeros(low.shape, table.dtype)
    for r in range(table.shape[0]):
        found = jnp.where(high == first_row + r, take_lanes(table[r : r + 1], low), found)
    return found


def each(count, step, unrolled):
    if unrolled:
        for i in range(count):
            step(i)
    else:

        def one(i, carry):
            step(i)
            return carry

        lax.fori_loop(0, count, one, 0)


def kernel(
    blocks,
    halves,
    ids_ref,
    real_ref,
    react_ref,
    volt_ref,
    rating_ref,
    mon_ref,
    out_ids_ref,
    pairs_ref,
    coup_ref,
    tiles_hbm,
    peak_ref,
    worst_ref,
    tiles,
    index,
    table_out,
    table_in,
    pair_out,
    pair_in,
    weights,
    columns,
    rows,
    squares,
    worst_out,
    worst_in,
    tile_sem,
    table_sems,
    pair_send,
    pair_recv,
    worst_send,
    worst_recv,
):
    devices = blocks * halves
    tiles_dev, slots, tile_size, _ = tiles_hbm.shape
    table_rows = real_ref.shape[0]
    unrolled = devices <= 16
    blk = lax.axis_index("blk")
    state = lax.axis_index("state")
    me = state * blocks + blk

    def place(i):
        other = lax.rem(me + i + 1, devices)
        return other, {"blk": lax.rem(other, blocks), "state": other // blocks}

    barrier = pltpu.get_barrier_semaphore()

    def greet(i):
        _, where_to = place(i)
        pl.semaphore_signal(barrier, inc=1, device_id=where_to, device_id_type=MESH)

    each(devices - 1, greet, unrolled)
    tile_copy = pltpu.make_async_copy(tiles_hbm, tiles, tile_sem)
    tile_copy.start()

    first, second = pairs_ref[0:1], pairs_ref[1:2]
    spot = lax.broadcasted_iota(jnp.int32, (tile_size, first.shape[1]), 0)
    at_first, at_second = spot == first, spot == second
    one, zero = jnp.float32(1.0), jnp.float32(0.0)
    picks = jnp.concatenate([jnp.where(at_second, one, zero), jnp.where(at_first, one, zero)], axis=1)
    picked = jnp.dot(coup_ref[...], picks.astype(jnp.bfloat16), preferred_element_type=jnp.float32)
    pair_count = first.shape[1]
    s_first_second = jnp.sum(jnp.where(at_first, picked[:, :pair_count], 0.0), axis=0, keepdims=True)
    s_second_first = jnp.sum(jnp.where(at_second, picked[:, pair_count:], 0.0), axis=0, keepdims=True)

    index[...] = jnp.zeros_like(index)
    index[0:tiles_dev] = mon_ref[...]
    out_ids = out_ids_ref[...]
    wide = (8, LANES)
    index[tiles_dev : tiles_dev + 1] = take_lanes(out_ids, jnp.broadcast_to(first, wide))[0:1]
    index[tiles_dev + 1 : tiles_dev + 2] = take_lanes(out_ids, jnp.broadcast_to(second, wide))[0:1]
    high, low = index[...] >> 7, index[...] & (LANES - 1)

    limit_own = volt_ref[...] * rating_ref[...]
    table_out[0] = real_ref[...]
    table_out[1] = react_ref[...]
    table_out[2] = limit_own
    own_row = state * table_rows
    real_own = lookup(real_ref[...], high, low, own_row)
    flows = real_own[tiles_dev : tiles_dev + 2].astype(jnp.bfloat16).astype(jnp.float32)
    is_first = state == 0
    pair_out[0:2] = flows
    pair_out[2:3] = jnp.where(is_first, first.astype(jnp.float32), s_first_second)
    pair_out[3:4] = jnp.where(is_first, second.astype(jnp.float32), s_second_first)

    pl.semaphore_wait(barrier, devices - 1)

    def pair_copy(i):
        other, where_to = place(i)
        return pltpu.make_async_remote_copy(
            src_ref=pair_out,
            dst_ref=pair_in.at[me],
            send_sem=pair_send.at[other],
            recv_sem=pair_recv.at[me],
            device_id=where_to,
            device_id_type=MESH,
        )

    table_copy = pltpu.make_async_remote_copy(
        src_ref=table_out,
        dst_ref=table_in,
        send_sem=table_sems.at[0],
        recv_sem=table_sems.at[1],
        device_id={"state": 1 - state},
        device_id_type=MESH,
    )
    each(devices - 1, lambda i: pair_copy(i).start(), unrolled)
    table_copy.start()
    pair_in[me] = pair_out[...]

    react_own = lookup(react_ref[...], high, low, own_row)
    limit_mine = lookup(limit_own, high, low, own_row)
    weights[0] = jnp.zeros(weights.shape[1:], weights.dtype)
    table_copy.wait_recv()
    other_row = (1 - state) * table_rows
    mine = (high >= own_row) & (high < own_row + table_rows)
    real = jnp.where(mine, real_own, lookup(table_in[0], high, low, other_row))
    react = jnp.where(mine, react_own, lookup(table_in[1], high, low, other_row))
    limit = jnp.where(mine, limit_mine, lookup(table_in[2], high, low, other_row))
    react_sq = react * react
    rows[0:8] = real
    rows[8:16] = react_sq
    rows[16:24] = 1.0 / (limit * limit)
    rows[24:] = jnp.zeros((rows.shape[0] - 24, LANES), jnp.float32)
    upright = rows[...].T
    for t in range(tiles_dev):
        for q in range(3):
            column = upright[:, 8 * q + t : 8 * q + t + 1]
            columns[t, q] = jnp.broadcast_to(column, (tile_size, pair_count))
    block_of = lax.broadcasted_iota(jnp.int32, (blocks, pair_count), 0)
    worst = jnp.zeros((blocks, pair_count), jnp.float32)
    for t in range(tiles_dev):
        base = columns[t, 0]
        base_peak = jnp.max((base * base + columns[t, 1]) * columns[t, 2], axis=0, keepdims=True)
        absent = block_of >= 0
        for k in range(slots):
            absent = absent & (block_of != ids_ref[t, k])
        worst = jnp.maximum(worst, jnp.where(absent, base_peak, 0.0))
    tile_copy.wait()

    def pair_arrived(i):
        other, where_to = place(i)
        pltpu.make_async_remote_copy(
            src_ref=pair_out,
            dst_ref=pair_in.at[other],
            send_sem=pair_send.at[other],
            recv_sem=pair_recv.at[other],
            device_id=where_to,
            device_id_type=MESH,
        ).wait_recv()

    each(devices - 1, pair_arrived, unrolled)
    flow_first = pair_in[0:blocks, 0] + pair_in[blocks:, 0]
    flow_second = pair_in[0:blocks, 1] + pair_in[blocks:, 1]
    first_all = pair_in[0:blocks, 2].astype(jnp.int32)
    second_all = pair_in[0:blocks, 3].astype(jnp.int32)
    s_fs, s_sf = pair_in[blocks:, 2], pair_in[blocks:, 3]
    determinant = 1.0 - s_fs * s_sf
    w_first = (flow_first + s_fs * flow_second) / determinant
    w_second = (flow_second + s_sf * flow_first) / determinant
    for b in range(blocks):
        one_row = slice(b, b + 1)
        weights[b + 1] = jnp.where(
            spot == first_all[one_row],
            w_first[one_row],
            jnp.where(spot == second_all[one_row], w_second[one_row], 0.0),
        ).astype(jnp.bfloat16)

    for t in range(tiles_dev):

        def one_slot(k, carried):
            most, worst = carried
            block = ids_ref[t, k]
            delta = jnp.dot(tiles[t, k], weights[block + 1], preferred_element_type=jnp.float32)
            post = columns[t, 0] + delta
            square = post * post
            ratio = (square + columns[t, 1]) * columns[t, 2]
            top = jnp.max(ratio, axis=0, keepdims=True)
            worst = jnp.where(block_of == block, jnp.maximum(worst, top), worst)
            return jnp.maximum(most, square), worst

        base = columns[t, 0]
        carried = (base * base, worst)
        if slots <= 4:
            for k in range(slots):
                carried = one_slot(k, carried)
        else:
            carried = lax.fori_loop(0, slots, one_slot, carried)
        most, worst = carried
        squares[t] = most
    worst_out[:, 0] = worst

    def worst_copy(i):
        other, where_to = place(i)
        return pltpu.make_async_remote_copy(
            src_ref=worst_out.at[where_to["blk"]],
            dst_ref=worst_in.at[me],
            send_sem=worst_send.at[other],
            recv_sem=worst_recv.at[me],
            device_id=where_to,
            device_id_type=MESH,
        )

    each(devices - 1, lambda i: worst_copy(i).start(), unrolled)
    worst_in[me] = worst_out[blk]
    for t in range(tiles_dev):
        most = jnp.max(squares[t].T, axis=0, keepdims=True)
        peak_ref[t : t + 1] = jnp.sqrt((most + rows[8 + t : 9 + t]) * rows[16 + t : 17 + t])

    def worst_arrived(i):
        other, where_to = place(i)
        pltpu.make_async_remote_copy(
            src_ref=worst_out.at[blk],
            dst_ref=worst_in.at[other],
            send_sem=worst_send.at[other],
            recv_sem=worst_recv.at[other],
            device_id=where_to,
            device_id_type=MESH,
        ).wait_recv()

    each(devices - 1, worst_arrived, unrolled)
    total = jnp.sqrt(jnp.max(worst_in[...], axis=0))
    half = pair_count // halves
    worst_ref[...] = jnp.where(is_first, total[:, :half], total[:, half:])

    table_copy.wait_send()

    def sent(i):
        pair_copy(i).wait_send()
        worst_copy(i).wait_send()

    each(devices - 1, sent, unrolled)


def body(
    base_real,
    base_reactive,
    voltage,
    rating,
    monitored,
    tile_ids,
    tile_values,
    outage_ids,
    coupling,
    outage_pairs,
):
    blocks = lax.axis_size("blk")
    halves = lax.axis_size("state")
    devices = blocks * halves
    tiles_dev, slots, tile_size, _ = tile_values.shape
    pair_count = outage_pairs.shape[2]
    table_rows = base_real.shape[0] // LANES
    vmem = pl.BlockSpec(memory_space=pltpu.VMEM)
    f32 = jnp.float32
    peak, worst = pl.pallas_call(
        functools.partial(kernel, blocks, halves),
        out_shape=(
            jax.ShapeDtypeStruct((tiles_dev, tile_size), f32),
            jax.ShapeDtypeStruct((1, pair_count // halves), f32),
        ),
        in_specs=[pl.BlockSpec(memory_space=pltpu.SMEM)]
        + [vmem] * 8
        + [pl.BlockSpec(memory_space=pl.ANY)],
        out_specs=(vmem, vmem),
        scratch_shapes=[
            pltpu.VMEM(tile_values.shape, tile_values.dtype),
            pltpu.VMEM((8, LANES), jnp.int32),
            pltpu.VMEM((3, table_rows, LANES), f32),
            pltpu.VMEM((3, table_rows, LANES), f32),
            pltpu.VMEM((4, pair_count), f32),
            pltpu.VMEM((devices, 4, pair_count), f32),
            pltpu.VMEM((blocks + 1, tile_size, pair_count), jnp.bfloat16),
            pltpu.VMEM((tiles_dev, 3, tile_size, pair_count), f32),
            pltpu.VMEM((LANES, LANES), f32),
            pltpu.VMEM((tiles_dev, tile_size, pair_count), f32),
            pltpu.VMEM((blocks, 1, pair_count), f32),
            pltpu.VMEM((devices, 1, pair_count), f32),
            pltpu.SemaphoreType.DMA(()),
            pltpu.SemaphoreType.DMA((2,)),
            pltpu.SemaphoreType.DMA((devices,)),
            pltpu.SemaphoreType.DMA((devices,)),
            pltpu.SemaphoreType.DMA((devices,)),
            pltpu.SemaphoreType.DMA((devices,)),
        ],
        compiler_params=pltpu.CompilerParams(
            collective_id=0, has_side_effects=True, vmem_limit_bytes=48 * 1024 * 1024
        ),
        name="screen",
    )(
        tile_ids,
        base_real.reshape(table_rows, LANES),
        base_reactive.reshape(table_rows, LANES),
        voltage.reshape(table_rows, LANES),
        rating.reshape(table_rows, LANES),
        monitored.reshape(tiles_dev, tile_size),
        outage_ids,
        outage_pairs[0],
        coupling[0],
        tile_values,
    )
    return peak.reshape(-1), worst


def solution(mesh):
    every = P(("cases", "blk", "state"))
    by_block = P(("cases", "blk"))
    return jax.shard_map(
        body,
        mesh=mesh,
        in_specs=(every,) * 7 + (by_block,) * 3,
        out_specs=(every, P(("cases", "blk"), "state")),
        check_vma=False,
    )
```

```python
import functools

import jax
import jax.numpy as jnp
from jax import lax
from jax.experimental import pallas as pl
from jax.experimental.pallas import tpu as pltpu
from jax.sharding import PartitionSpec as P

MESH = pl.DeviceIdType.MESH
LANES = 128


def take_lanes(row, lanes):
    spread = jnp.broadcast_to(row, lanes.shape)
    return jnp.take_along_axis(spread, lanes, axis=1, mode="promise_in_bounds")


def lookup(table, high, low, first_row):
    found = jnp.zeros(low.shape, table.dtype)
    for r in range(table.shape[0]):
        found = jnp.where(high == first_row + r, take_lanes(table[r : r + 1], low), found)
    return found


def each(count, step, unrolled):
    if unrolled:
        for i in range(count):
            step(i)
    else:

        def one(i, carry):
            step(i)
            return carry

        lax.fori_loop(0, count, one, 0)


def kernel(
    blocks,
    halves,
    pairs_hbm,
    coup_hbm,
    out_ids_hbm,
    real_hbm,
    mon_hbm,
    react_hbm,
    volt_hbm,
    rating_hbm,
    ids_hbm,
    tiles_hbm,
    out_ref,
    pairs_ref,
    coup_ref,
    out_ids_ref,
    real_ref,
    mon_ref,
    react_ref,
    volt_ref,
    rating_ref,
    ids_ref,
    tiles,
    index,
    table_out,
    table_in,
    pair_out,
    pair_in,
    weights,
    columns,
    rows,
    squares,
    worst_out,
    worst_in,
    load_sems,
    table_sems,
    pair_send,
    pair_recv,
    worst_send,
    worst_recv,
):
    devices = blocks * halves
    tiles_dev, slots, tile_size, _ = tiles_hbm.shape
    table_rows = real_ref.shape[0]
    unrolled = devices <= 16
    blk = lax.axis_index("blk")
    state = lax.axis_index("state")
    me = state * blocks + blk

    def place(i):
        other = lax.rem(me + i + 1, devices)
        return other, {"blk": lax.rem(other, blocks), "state": other // blocks}

    loads = [
        pltpu.make_async_copy(source, target, load_sems.at[i])
        for i, (source, target) in enumerate(
            (
                (pairs_hbm, pairs_ref),
                (coup_hbm, coup_ref),
                (out_ids_hbm, out_ids_ref),
                (real_hbm, real_ref),
                (mon_hbm, mon_ref),
                (react_hbm, react_ref),
                (volt_hbm, volt_ref),
                (rating_hbm, rating_ref),
                (ids_hbm, ids_ref),
                (tiles_hbm, tiles),
            )
        )
    ]
    for load in loads[:8]:
        load.start()
    barrier = pltpu.get_barrier_semaphore()

    def greet(i):
        _, where_to = place(i)
        pl.semaphore_signal(barrier, inc=1, device_id=where_to, device_id_type=MESH)

    each(devices - 1, greet, unrolled)
    for load in loads[8:]:
        load.start()
    for load in loads[:8]:
        load.wait()

    first, second = pairs_ref[0:1], pairs_ref[1:2]
    spot = lax.broadcasted_iota(jnp.int32, (tile_size, first.shape[1]), 0)
    at_first, at_second = spot == first, spot == second
    one, zero = jnp.float32(1.0), jnp.float32(0.0)
    picks = jnp.concatenate([jnp.where(at_second, one, zero), jnp.where(at_first, one, zero)], axis=1)
    picked = jnp.dot(coup_ref[...], picks.astype(jnp.bfloat16), preferred_element_type=jnp.float32)
    pair_count = first.shape[1]
    s_first_second = jnp.sum(jnp.where(at_first, picked[:, :pair_count], 0.0), axis=0, keepdims=True)
    s_second_first = jnp.sum(jnp.where(at_second, picked[:, pair_count:], 0.0), axis=0, keepdims=True)

    index[...] = jnp.zeros_like(index)
    index[0:tiles_dev] = mon_ref[...]
    out_ids = out_ids_ref[...]
    wide = (8, LANES)
    index[tiles_dev : tiles_dev + 1] = take_lanes(out_ids, jnp.broadcast_to(first, wide))[0:1]
    index[tiles_dev + 1 : tiles_dev + 2] = take_lanes(out_ids, jnp.broadcast_to(second, wide))[0:1]
    high, low = index[...] >> 7, index[...] & (LANES - 1)

    limit_own = volt_ref[...] * rating_ref[...]
    table_out[0] = real_ref[...]
    table_out[1] = react_ref[...]
    table_out[2] = limit_own
    own_row = state * table_rows
    real_own = lookup(real_ref[...], high, low, own_row)
    flows = real_own[tiles_dev : tiles_dev + 2].astype(jnp.bfloat16).astype(jnp.float32)
    is_first = state == 0
    pair_out[0:2] = flows
    pair_out[2:3] = jnp.where(is_first, first.astype(jnp.float32), s_first_second)
    pair_out[3:4] = jnp.where(is_first, second.astype(jnp.float32), s_second_first)

    pl.semaphore_wait(barrier, devices - 1)

    def pair_copy(i):
        other, where_to = place(i)
        return pltpu.make_async_remote_copy(
            src_ref=pair_out,
            dst_ref=pair_in.at[me],
            send_sem=pair_send.at[other],
            recv_sem=pair_recv.at[me],
            device_id=where_to,
            device_id_type=MESH,
        )

    table_copy = pltpu.make_async_remote_copy(
        src_ref=table_out,
        dst_ref=table_in,
        send_sem=table_sems.at[0],
        recv_sem=table_sems.at[1],
        device_id={"state": 1 - state},
        device_id_type=MESH,
    )
    each(devices - 1, lambda i: pair_copy(i).start(), unrolled)
    table_copy.start()
    pair_in[me] = pair_out[...]

    react_own = lookup(react_ref[...], high, low, own_row)
    limit_mine = lookup(limit_own, high, low, own_row)
    weights[0] = jnp.zeros(weights.shape[1:], weights.dtype)
    table_copy.wait_recv()
    other_row = (1 - state) * table_rows
    mine = (high >= own_row) & (high < own_row + table_rows)
    real = jnp.where(mine, real_own, lookup(table_in[0], high, low, other_row))
    react = jnp.where(mine, react_own, lookup(table_in[1], high, low, other_row))
    limit = jnp.where(mine, limit_mine, lookup(table_in[2], high, low, other_row))
    react_sq = react * react
    rows[0:8] = real
    rows[8:16] = react_sq
    rows[16:24] = 1.0 / (limit * limit)
    rows[24:] = jnp.zeros((rows.shape[0] - 24, LANES), jnp.float32)
    upright = rows[...].T
    for t in range(tiles_dev):
        for q in range(3):
            column = upright[:, 8 * q + t : 8 * q + t + 1]
            columns[t, q] = jnp.broadcast_to(column, (tile_size, pair_count))
    loads[8].wait()
    block_of = lax.broadcasted_iota(jnp.int32, (blocks, pair_count), 0)
    worst = jnp.zeros((blocks, pair_count), jnp.float32)
    for t in range(tiles_dev):
        base = columns[t, 0]
        base_peak = jnp.max((base * base + columns[t, 1]) * columns[t, 2], axis=0, keepdims=True)
        absent = block_of >= 0
        for k in range(slots):
            absent = absent & (block_of != ids_ref[t, k])
        worst = jnp.maximum(worst, jnp.where(absent, base_peak, 0.0))
    loads[9].wait()

    def pair_arrived(i):
        other, where_to = place(i)
        pltpu.make_async_remote_copy(
            src_ref=pair_out,
            dst_ref=pair_in.at[other],
            send_sem=pair_send.at[other],
            recv_sem=pair_recv.at[other],
            device_id=where_to,
            device_id_type=MESH,
        ).wait_recv()

    each(devices - 1, pair_arrived, unrolled)
    flow_first = pair_in[0:blocks, 0] + pair_in[blocks:, 0]
    flow_second = pair_in[0:blocks, 1] + pair_in[blocks:, 1]
    first_all = pair_in[0:blocks, 2].astype(jnp.int32)
    second_all = pair_in[0:blocks, 3].astype(jnp.int32)
    s_fs, s_sf = pair_in[blocks:, 2], pair_in[blocks:, 3]
    determinant = 1.0 - s_fs * s_sf
    w_first = (flow_first + s_fs * flow_second) / determinant
    w_second = (flow_second + s_sf * flow_first) / determinant
    for b in range(blocks):
        one_row = slice(b, b + 1)
        weights[b + 1] = jnp.where(
            spot == first_all[one_row],
            w_first[one_row],
            jnp.where(spot == second_all[one_row], w_second[one_row], 0.0),
        ).astype(jnp.bfloat16)

    for t in range(tiles_dev):

        def one_slot(k, carried):
            most, worst = carried
            block = ids_ref[t, k]
            delta = jnp.dot(tiles[t, k], weights[block + 1], preferred_element_type=jnp.float32)
            post = columns[t, 0] + delta
            square = post * post
            ratio = (square + columns[t, 1]) * columns[t, 2]
            top = jnp.max(ratio, axis=0, keepdims=True)
            worst = jnp.where(block_of == block, jnp.maximum(worst, top), worst)
            return jnp.maximum(most, square), worst

        base = columns[t, 0]
        carried = (base * base, worst)
        if slots <= 4:
            for k in range(slots):
                carried = one_slot(k, carried)
        else:
            carried = lax.fori_loop(0, slots, one_slot, carried)
        most, worst = carried
        squares[t] = most
    worst_out[:, 0] = worst

    def worst_copy(i):
        other, where_to = place(i)
        return pltpu.make_async_remote_copy(
            src_ref=worst_out.at[where_to["blk"]],
            dst_ref=worst_in.at[me],
            send_sem=worst_send.at[other],
            recv_sem=worst_recv.at[me],
            device_id=where_to,
            device_id_type=MESH,
        )

    each(devices - 1, lambda i: worst_copy(i).start(), unrolled)
    worst_in[me] = worst_out[blk]
    for t in range(tiles_dev):
        most = jnp.max(squares[t].T, axis=0, keepdims=True)
        out_ref[t : t + 1] = jnp.sqrt((most + rows[8 + t : 9 + t]) * rows[16 + t : 17 + t])

    def worst_arrived(i):
        other, where_to = place(i)
        pltpu.make_async_remote_copy(
            src_ref=worst_out.at[blk],
            dst_ref=worst_in.at[other],
            send_sem=worst_send.at[other],
            recv_sem=worst_recv.at[other],
            device_id=where_to,
            device_id_type=MESH,
        ).wait_recv()

    each(devices - 1, worst_arrived, unrolled)
    total = jnp.sqrt(jnp.max(worst_in[...], axis=0))
    half = pair_count // halves
    out_ref[tiles_dev : tiles_dev + 1, :half] = jnp.where(is_first, total[:, :half], total[:, half:])

    table_copy.wait_send()

    def sent(i):
        pair_copy(i).wait_send()
        worst_copy(i).wait_send()

    each(devices - 1, sent, unrolled)


def body(
    base_real,
    base_reactive,
    voltage,
    rating,
    monitored,
    tile_ids,
    tile_values,
    outage_ids,
    coupling,
    outage_pairs,
):
    blocks = lax.axis_size("blk")
    halves = lax.axis_size("state")
    devices = blocks * halves
    tiles_dev, slots, tile_size, _ = tile_values.shape
    pair_count = outage_pairs.shape[2]
    table_rows = base_real.shape[0] // LANES
    f32 = jnp.float32
    operands = (
        outage_pairs[0],
        coupling[0],
        outage_ids,
        base_real.reshape(table_rows, LANES),
        monitored.reshape(tiles_dev, tile_size),
        base_reactive.reshape(table_rows, LANES),
        voltage.reshape(table_rows, LANES),
        rating.reshape(table_rows, LANES),
        tile_ids,
        tile_values,
    )
    spaces = [pltpu.VMEM] * 8 + [pltpu.SMEM, pltpu.VMEM]
    results = pl.pallas_call(
        functools.partial(kernel, blocks, halves),
        out_shape=jax.ShapeDtypeStruct((8, LANES), f32),
        in_specs=[pl.BlockSpec(memory_space=pltpu.HBM)] * 10,
        out_specs=pl.BlockSpec(memory_space=pltpu.VMEM),
        scratch_shapes=[space(x.shape, x.dtype) for space, x in zip(spaces, operands)]
        + [
            pltpu.VMEM((8, LANES), jnp.int32),
            pltpu.VMEM((3, table_rows, LANES), f32),
            pltpu.VMEM((3, table_rows, LANES), f32),
            pltpu.VMEM((4, pair_count), f32),
            pltpu.VMEM((devices, 4, pair_count), f32),
            pltpu.VMEM((blocks + 1, tile_size, pair_count), jnp.bfloat16),
            pltpu.VMEM((tiles_dev, 3, tile_size, pair_count), f32),
            pltpu.VMEM((LANES, LANES), f32),
            pltpu.VMEM((tiles_dev, tile_size, pair_count), f32),
            pltpu.VMEM((blocks, 1, pair_count), f32),
            pltpu.VMEM((devices, 1, pair_count), f32),
            pltpu.SemaphoreType.DMA((10,)),
            pltpu.SemaphoreType.DMA((2,)),
            pltpu.SemaphoreType.DMA((devices,)),
            pltpu.SemaphoreType.DMA((devices,)),
            pltpu.SemaphoreType.DMA((devices,)),
            pltpu.SemaphoreType.DMA((devices,)),
        ],
        compiler_params=pltpu.CompilerParams(
            collective_id=0, has_side_effects=True, vmem_limit_bytes=64 * 1024 * 1024
        ),
        name="screen",
    )(*operands)
    peak = results[:tiles_dev].reshape(-1)
    worst = results[tiles_dev : tiles_dev + 1, : pair_count // halves]
    return peak, worst


def solution(mesh):
    every = P(("cases", "blk", "state"))
    by_block = P(("cases", "blk"))
    return jax.shard_map(
        body,
        mesh=mesh,
        in_specs=(every,) * 7 + (by_block,) * 3,
        out_specs=(every, P(("cases", "blk"), "state")),
        check_vma=False,
    )
```

```python
import functools

import jax
import jax.numpy as jnp
from jax import lax
from jax.experimental import pallas as pl
from jax.experimental.pallas import tpu as pltpu
from jax.sharding import PartitionSpec as P

MESH = pl.DeviceIdType.MESH
LANES = 128


def take_lanes(row, lanes):
    spread = jnp.broadcast_to(row, lanes.shape)
    return jnp.take_along_axis(spread, lanes, axis=1, mode="promise_in_bounds")


def lookup(table, high, low, first_row):
    found = jnp.zeros(low.shape, table.dtype)
    for r in range(table.shape[0]):
        found = jnp.where(high == first_row + r, take_lanes(table[r : r + 1], low), found)
    return found


def each(count, step, unrolled):
    if unrolled:
        for i in range(count):
            step(i)
    else:

        def one(i, carry):
            step(i)
            return carry

        lax.fori_loop(0, count, one, 0)


def kernel(
    blocks,
    halves,
    pairs_hbm,
    coup_hbm,
    out_ids_hbm,
    real_hbm,
    mon_hbm,
    react_hbm,
    volt_hbm,
    rating_hbm,
    ids_hbm,
    tiles_hbm,
    out_ref,
    pairs_ref,
    coup_ref,
    out_ids_ref,
    real_ref,
    mon_ref,
    react_ref,
    volt_ref,
    rating_ref,
    ids_ref,
    tiles,
    index,
    table_out,
    table_in,
    pair_out,
    pair_in,
    weights,
    columns,
    rows,
    squares,
    worst_out,
    worst_in,
    load_sems,
    table_sems,
    pair_send,
    pair_recv,
    worst_send,
    worst_recv,
):
    devices = blocks * halves
    tiles_dev, slots, tile_size, _ = tiles_hbm.shape
    table_rows = real_ref.shape[0]
    unrolled = devices <= 16
    blk = lax.axis_index("blk")
    state = lax.axis_index("state")
    me = state * blocks + blk

    def place(i):
        other = lax.rem(me + i + 1, devices)
        return other, {"blk": lax.rem(other, blocks), "state": other // blocks}

    loads = [
        pltpu.make_async_copy(source, target, load_sems.at[i])
        for i, (source, target) in enumerate(
            (
                (pairs_hbm, pairs_ref),
                (coup_hbm, coup_ref),
                (out_ids_hbm, out_ids_ref),
                (real_hbm, real_ref),
                (mon_hbm, mon_ref),
                (react_hbm, react_ref),
                (volt_hbm, volt_ref),
                (rating_hbm, rating_ref),
                (ids_hbm, ids_ref),
                (tiles_hbm, tiles),
            )
        )
    ]
    for load in loads[:8]:
        load.start()
    barrier = pltpu.get_barrier_semaphore()

    def greet(i):
        _, where_to = place(i)
        pl.semaphore_signal(barrier, inc=1, device_id=where_to, device_id_type=MESH)

    each(devices - 1, greet, unrolled)
    for load in loads[8:]:
        load.start()
    for load in loads[:8]:
        load.wait()

    first, second = pairs_ref[0:1], pairs_ref[1:2]
    spot = lax.broadcasted_iota(jnp.int32, (tile_size, first.shape[1]), 0)
    at_first, at_second = spot == first, spot == second
    one, zero = jnp.float32(1.0), jnp.float32(0.0)
    picks = jnp.concatenate([jnp.where(at_second, one, zero), jnp.where(at_first, one, zero)], axis=1)
    picked = jnp.dot(coup_ref[...], picks.astype(jnp.bfloat16), preferred_element_type=jnp.float32)
    pair_count = first.shape[1]
    s_first_second = jnp.sum(jnp.where(at_first, picked[:, :pair_count], 0.0), axis=0, keepdims=True)
    s_second_first = jnp.sum(jnp.where(at_second, picked[:, pair_count:], 0.0), axis=0, keepdims=True)

    index[...] = jnp.zeros_like(index)
    index[0:tiles_dev] = mon_ref[...]
    out_ids = out_ids_ref[...]
    wide = (8, LANES)
    index[tiles_dev : tiles_dev + 1] = take_lanes(out_ids, jnp.broadcast_to(first, wide))[0:1]
    index[tiles_dev + 1 : tiles_dev + 2] = take_lanes(out_ids, jnp.broadcast_to(second, wide))[0:1]
    high, low = index[...] >> 7, index[...] & (LANES - 1)

    limit_own = volt_ref[...] * rating_ref[...]
    table_out[0] = real_ref[...]
    table_out[1] = react_ref[...]
    table_out[2] = limit_own
    own_row = state * table_rows
    real_own = lookup(real_ref[...], high, low, own_row)
    flows = real_own[tiles_dev : tiles_dev + 2].astype(jnp.bfloat16).astype(jnp.float32)
    is_first = state == 0
    pair_out[0:2] = flows
    pair_out[2:3] = jnp.where(is_first, first.astype(jnp.float32), s_first_second)
    pair_out[3:4] = jnp.where(is_first, second.astype(jnp.float32), s_second_first)

    pl.semaphore_wait(barrier, devices - 1)

    def pair_copy(i):
        _, where_to = place(i)
        return pltpu.make_async_remote_copy(
            src_ref=pair_out,
            dst_ref=pair_in.at[me],
            send_sem=pair_send,
            recv_sem=pair_recv,
            device_id=where_to,
            device_id_type=MESH,
        )

    table_copy = pltpu.make_async_remote_copy(
        src_ref=table_out,
        dst_ref=table_in,
        send_sem=table_sems.at[0],
        recv_sem=table_sems.at[1],
        device_id={"state": 1 - state},
        device_id_type=MESH,
    )
    table_copy.start()
    each(devices - 1, lambda i: pair_copy(i).start(), unrolled)
    pair_in[me] = pair_out[...]

    react_own = lookup(react_ref[...], high, low, own_row)
    limit_mine = lookup(limit_own, high, low, own_row)
    weights[0] = jnp.zeros(weights.shape[1:], weights.dtype)
    table_copy.wait_recv()
    other_row = (1 - state) * table_rows
    mine = (high >= own_row) & (high < own_row + table_rows)
    real = jnp.where(mine, real_own, lookup(table_in[0], high, low, other_row))
    react = jnp.where(mine, react_own, lookup(table_in[1], high, low, other_row))
    limit = jnp.where(mine, limit_mine, lookup(table_in[2], high, low, other_row))
    react_sq = react * react
    rows[0:8] = real
    rows[8:16] = react_sq
    rows[16:24] = 1.0 / (limit * limit)
    rows[24:] = jnp.zeros((rows.shape[0] - 24, LANES), jnp.float32)
    upright = rows[...].T
    for t in range(tiles_dev):
        for q in range(3):
            column = upright[:, 8 * q + t : 8 * q + t + 1]
            columns[t, q] = jnp.broadcast_to(column, (tile_size, pair_count))
    loads[8].wait()
    block_of = lax.broadcasted_iota(jnp.int32, (blocks, pair_count), 0)
    worst = jnp.zeros((blocks, pair_count), jnp.float32)
    for t in range(tiles_dev):
        base = columns[t, 0]
        base_peak = jnp.max((base * base + columns[t, 1]) * columns[t, 2], axis=0, keepdims=True)
        absent = block_of >= 0
        for k in range(slots):
            absent = absent & (block_of != ids_ref[t, k])
        worst = jnp.maximum(worst, jnp.where(absent, base_peak, 0.0))
    loads[9].wait()

    peers = pl.ds(0, devices - 1)
    pltpu.make_async_copy(pair_in.at[peers], pair_in.at[peers], pair_recv).wait()
    flow_first = pair_in[0:blocks, 0] + pair_in[blocks:, 0]
    flow_second = pair_in[0:blocks, 1] + pair_in[blocks:, 1]
    first_all = pair_in[0:blocks, 2].astype(jnp.int32)
    second_all = pair_in[0:blocks, 3].astype(jnp.int32)
    s_fs, s_sf = pair_in[blocks:, 2], pair_in[blocks:, 3]
    determinant = 1.0 - s_fs * s_sf
    w_first = (flow_first + s_fs * flow_second) / determinant
    w_second = (flow_second + s_sf * flow_first) / determinant
    for b in range(blocks):
        one_row = slice(b, b + 1)
        weights[b + 1] = jnp.where(
            spot == first_all[one_row],
            w_first[one_row],
            jnp.where(spot == second_all[one_row], w_second[one_row], 0.0),
        ).astype(jnp.bfloat16)

    for t in range(tiles_dev):

        def one_slot(k, carried):
            most, worst = carried
            block = ids_ref[t, k]
            delta = jnp.dot(tiles[t, k], weights[block + 1], preferred_element_type=jnp.float32)
            post = columns[t, 0] + delta
            square = post * post
            ratio = (square + columns[t, 1]) * columns[t, 2]
            top = jnp.max(ratio, axis=0, keepdims=True)
            worst = jnp.where(block_of == block, jnp.maximum(worst, top), worst)
            return jnp.maximum(most, square), worst

        base = columns[t, 0]
        carried = (base * base, worst)
        if slots <= 4:
            for k in range(slots):
                carried = one_slot(k, carried)
        else:
            carried = lax.fori_loop(0, slots, one_slot, carried)
        most, worst = carried
        squares[t] = most
    worst_out[:, 0] = worst

    def worst_copy(i):
        _, where_to = place(i)
        return pltpu.make_async_remote_copy(
            src_ref=worst_out.at[where_to["blk"]],
            dst_ref=worst_in.at[me],
            send_sem=worst_send,
            recv_sem=worst_recv,
            device_id=where_to,
            device_id_type=MESH,
        )

    each(devices - 1, lambda i: worst_copy(i).start(), unrolled)
    worst_in[me] = worst_out[blk]
    for t in range(tiles_dev):
        most = jnp.max(squares[t].T, axis=0, keepdims=True)
        out_ref[t : t + 1] = jnp.sqrt((most + rows[8 + t : 9 + t]) * rows[16 + t : 17 + t])

    table_copy.wait_send()
    pltpu.make_async_copy(pair_in.at[peers], pair_in.at[peers], pair_send).wait()
    pltpu.make_async_copy(worst_in.at[peers], worst_in.at[peers], worst_send).wait()
    pltpu.make_async_copy(worst_in.at[peers], worst_in.at[peers], worst_recv).wait()
    total = jnp.sqrt(jnp.max(worst_in[...], axis=0))
    half = pair_count // halves
    out_ref[tiles_dev : tiles_dev + 1, :half] = jnp.where(is_first, total[:, :half], total[:, half:])


def body(
    base_real,
    base_reactive,
    voltage,
    rating,
    monitored,
    tile_ids,
    tile_values,
    outage_ids,
    coupling,
    outage_pairs,
):
    blocks = lax.axis_size("blk")
    halves = lax.axis_size("state")
    devices = blocks * halves
    tiles_dev, slots, tile_size, _ = tile_values.shape
    pair_count = outage_pairs.shape[2]
    table_rows = base_real.shape[0] // LANES
    f32 = jnp.float32
    operands = (
        outage_pairs[0],
        coupling[0],
        outage_ids,
        base_real.reshape(table_rows, LANES),
        monitored.reshape(tiles_dev, tile_size),
        base_reactive.reshape(table_rows, LANES),
        voltage.reshape(table_rows, LANES),
        rating.reshape(table_rows, LANES),
        tile_ids,
        tile_values,
    )
    spaces = [pltpu.VMEM] * 8 + [pltpu.SMEM, pltpu.VMEM]
    results = pl.pallas_call(
        functools.partial(kernel, blocks, halves),
        out_shape=jax.ShapeDtypeStruct((8, LANES), f32),
        in_specs=[pl.BlockSpec(memory_space=pltpu.HBM)] * 10,
        out_specs=pl.BlockSpec(memory_space=pltpu.VMEM),
        scratch_shapes=[space(x.shape, x.dtype) for space, x in zip(spaces, operands)]
        + [
            pltpu.VMEM((8, LANES), jnp.int32),
            pltpu.VMEM((3, table_rows, LANES), f32),
            pltpu.VMEM((3, table_rows, LANES), f32),
            pltpu.VMEM((4, pair_count), f32),
            pltpu.VMEM((devices, 4, pair_count), f32),
            pltpu.VMEM((blocks + 1, tile_size, pair_count), jnp.bfloat16),
            pltpu.VMEM((tiles_dev, 3, tile_size, pair_count), f32),
            pltpu.VMEM((LANES, LANES), f32),
            pltpu.VMEM((tiles_dev, tile_size, pair_count), f32),
            pltpu.VMEM((blocks, 1, pair_count), f32),
            pltpu.VMEM((devices, 1, pair_count), f32),
            pltpu.SemaphoreType.DMA((10,)),
            pltpu.SemaphoreType.DMA((2,)),
            pltpu.SemaphoreType.DMA(()),
            pltpu.SemaphoreType.DMA(()),
            pltpu.SemaphoreType.DMA(()),
            pltpu.SemaphoreType.DMA(()),
        ],
        compiler_params=pltpu.CompilerParams(
            collective_id=0, has_side_effects=True, vmem_limit_bytes=48 * 1024 * 1024
        ),
        name="screen",
    )(*[pltpu.with_memory_space_constraint(x, pltpu.HBM) for x in operands])
    peak = results[:tiles_dev].reshape(-1)
    worst = results[tiles_dev : tiles_dev + 1, : pair_count // halves]
    return peak, worst


def solution(mesh):
    every = P(("cases", "blk", "state"))
    by_block = P(("cases", "blk"))
    return jax.shard_map(
        body,
        mesh=mesh,
        in_specs=(every,) * 7 + (by_block,) * 3,
        out_specs=(every, P(("cases", "blk"), "state")),
        check_vma=False,
    )
```

```python
import functools

import jax
import jax.numpy as jnp
from jax import lax
from jax.experimental import pallas as pl
from jax.experimental.pallas import tpu as pltpu
from jax.sharding import PartitionSpec as P

MESH = pl.DeviceIdType.MESH
LANES = 128


def take_lanes(row, lanes):
    spread = jnp.broadcast_to(row, lanes.shape)
    return jnp.take_along_axis(spread, lanes, axis=1, mode="promise_in_bounds")


def lookup(table, high, low, first_row):
    found = jnp.zeros(low.shape, table.dtype)
    for r in range(table.shape[0]):
        found = jnp.where(high == first_row + r, take_lanes(table[r : r + 1], low), found)
    return found


def kernel(
    blocks,
    halves,
    pairs_hbm,
    coup_hbm,
    out_ids_hbm,
    real_hbm,
    mon_hbm,
    react_hbm,
    volt_hbm,
    rating_hbm,
    ids_hbm,
    tiles_hbm,
    peak_ref,
    worst_ref,
    pairs_ref,
    coup_ref,
    out_ids_ref,
    real_ref,
    mon_ref,
    react_ref,
    volt_ref,
    rating_ref,
    ids_ref,
    tiles,
    index,
    table_out,
    table_in,
    pair_out,
    pair_in,
    weights,
    columns,
    rows,
    pair_rows,
    squares,
    tops,
    worst_out,
    worst_in,
    load_sems,
    table_sems,
    pair_send,
    pair_recv,
    worst_send,
    worst_recv,
):
    devices = blocks * halves
    tiles_dev, slots, tile_size, _ = tiles_hbm.shape
    table_rows = real_ref.shape[0]
    blk = lax.axis_index("blk")
    state = lax.axis_index("state")
    me = state * blocks + blk

    def each_peer(step):
        step(blk, 1 - state)

        def one_block(i, carry):
            turned = blk + i
            to = jnp.where(turned >= blocks, turned - blocks, turned)
            step(to, state)
            step(to, 1 - state)
            return carry

        lax.fori_loop(1, blocks, one_block, 0)

    loads = [
        pltpu.make_async_copy(source, target, load_sems.at[i])
        for i, (source, target) in enumerate(
            (
                (pairs_hbm, pairs_ref),
                (coup_hbm, coup_ref),
                (out_ids_hbm, out_ids_ref),
                (real_hbm, real_ref),
                (mon_hbm, mon_ref),
                (react_hbm, react_ref),
                (volt_hbm, volt_ref),
                (rating_hbm, rating_ref),
                (ids_hbm, ids_ref),
                (tiles_hbm, tiles),
            )
        )
    ]
    for load in loads[:8]:
        load.start()
    barrier = pltpu.get_barrier_semaphore()

    def greet(to, half):
        there = {"blk": to, "state": half}
        pl.semaphore_signal(barrier, inc=1, device_id=there, device_id_type=MESH)

    each_peer(greet)
    for load in loads[8:]:
        load.start()
    for load in loads[:8]:
        load.wait()

    first, second = pairs_ref[0:1], pairs_ref[1:2]
    spot = lax.broadcasted_iota(jnp.int32, (tile_size, first.shape[1]), 0)
    at_first, at_second = spot == first, spot == second
    one, zero = jnp.float32(1.0), jnp.float32(0.0)
    picks = jnp.concatenate([jnp.where(at_second, one, zero), jnp.where(at_first, one, zero)], axis=1)
    picked = jnp.dot(coup_ref[...], picks.astype(jnp.bfloat16), preferred_element_type=jnp.float32)
    pair_count = first.shape[1]
    s_first_second = jnp.sum(jnp.where(at_first, picked[:, :pair_count], 0.0), axis=0, keepdims=True)
    s_second_first = jnp.sum(jnp.where(at_second, picked[:, pair_count:], 0.0), axis=0, keepdims=True)

    index[...] = jnp.zeros_like(index)
    index[0:tiles_dev] = mon_ref[...]
    out_ids = out_ids_ref[...]
    wide = (8, LANES)
    index[tiles_dev : tiles_dev + 1] = take_lanes(out_ids, jnp.broadcast_to(first, wide))[0:1]
    index[tiles_dev + 1 : tiles_dev + 2] = take_lanes(out_ids, jnp.broadcast_to(second, wide))[0:1]
    high, low = index[...] >> 7, index[...] & (LANES - 1)

    limit_own = volt_ref[...] * rating_ref[...]
    table_out[0] = real_ref[...]
    table_out[1] = react_ref[...]
    table_out[2] = limit_own
    own_row = state * table_rows
    real_own = lookup(real_ref[...], high, low, own_row)
    flows = real_own[tiles_dev : tiles_dev + 2].astype(jnp.bfloat16).astype(jnp.float32)
    is_first = state == 0
    pair_out[0:2] = flows
    pair_out[2:3] = jnp.where(is_first, first.astype(jnp.float32), s_first_second)
    pair_out[3:4] = jnp.where(is_first, second.astype(jnp.float32), s_second_first)

    pl.semaphore_wait(barrier, devices - 1)

    def send_pairs(to, half):
        pltpu.make_async_remote_copy(
            src_ref=pair_out,
            dst_ref=pair_in.at[me],
            send_sem=pair_send,
            recv_sem=pair_recv,
            device_id={"blk": to, "state": half},
            device_id_type=MESH,
        ).start()

    table_copy = pltpu.make_async_remote_copy(
        src_ref=table_out,
        dst_ref=table_in,
        send_sem=table_sems.at[0],
        recv_sem=table_sems.at[1],
        device_id={"state": 1 - state},
        device_id_type=MESH,
    )
    table_copy.start()
    each_peer(send_pairs)
    pair_in[me] = pair_out[...]

    react_own = lookup(react_ref[...], high, low, own_row)
    limit_mine = lookup(limit_own, high, low, own_row)
    weights[0] = jnp.zeros(weights.shape[1:], weights.dtype)
    table_copy.wait_recv()
    other_row = (1 - state) * table_rows
    mine = (high >= own_row) & (high < own_row + table_rows)
    real = jnp.where(mine, real_own, lookup(table_in[0], high, low, other_row))
    react = jnp.where(mine, react_own, lookup(table_in[1], high, low, other_row))
    limit = jnp.where(mine, limit_mine, lookup(table_in[2], high, low, other_row))
    react_sq = react * react
    rows[0:8] = real
    rows[8:16] = react_sq
    rows[16:24] = 1.0 / (limit * limit)
    rows[24:] = jnp.zeros((rows.shape[0] - 24, LANES), jnp.float32)
    upright = rows[...].T
    for t in range(tiles_dev):
        for q in range(3):
            column = upright[:, 8 * q + t : 8 * q + t + 1]
            columns[t, q] = jnp.broadcast_to(column, (tile_size, pair_count))
    loads[8].wait()
    block_of = lax.broadcasted_iota(jnp.int32, (blocks, pair_count), 0)

    def base_tile(t, worst):
        base = columns[t, 0]
        base_peak = jnp.max((base * base + columns[t, 1]) * columns[t, 2], axis=0, keepdims=True)
        absent = block_of >= 0
        for k in range(slots):
            absent = absent & (block_of != ids_ref[t, k])
        return jnp.maximum(worst, jnp.where(absent, base_peak, 0.0))

    worst = lax.fori_loop(0, tiles_dev, base_tile, jnp.zeros((blocks, pair_count), jnp.float32))
    loads[9].wait()

    peers = pl.ds(0, devices - 1)
    pltpu.make_async_copy(pair_in.at[peers], pair_in.at[peers], pair_recv).wait()
    flow_first = pair_in[0:blocks, 0] + pair_in[blocks:, 0]
    flow_second = pair_in[0:blocks, 1] + pair_in[blocks:, 1]
    s_fs, s_sf = pair_in[blocks:, 2], pair_in[blocks:, 3]
    determinant = 1.0 - s_fs * s_sf
    w_first = (flow_first + s_fs * flow_second) / determinant
    w_second = (flow_second + s_sf * flow_first) / determinant
    pair_rows[0] = pair_in[0:blocks, 2]
    pair_rows[1] = pair_in[0:blocks, 3]
    pair_rows[2] = w_first
    pair_rows[3] = w_second
    place = spot.astype(jnp.float32)

    def build(b, carry):
        one_row = pl.ds(b, 1)
        weights[b + 1] = jnp.where(
            place == pair_rows[0, one_row],
            pair_rows[2, one_row],
            jnp.where(place == pair_rows[1, one_row], pair_rows[3, one_row], 0.0),
        ).astype(jnp.bfloat16)
        return carry

    lax.fori_loop(0, blocks, build, 0)

    def one_tile(t, worst):
        def one_slot(k, carried):
            most, worst = carried
            block = ids_ref[t, k]
            delta = jnp.dot(tiles[t, k], weights[block + 1], preferred_element_type=jnp.float32)
            post = columns[t, 0] + delta
            square = post * post
            ratio = (square + columns[t, 1]) * columns[t, 2]
            top = jnp.max(ratio, axis=0, keepdims=True)
            worst = jnp.where(block_of == block, jnp.maximum(worst, top), worst)
            return jnp.maximum(most, square), worst

        base = columns[t, 0]
        carried = (base * base, worst)
        if slots <= 4:
            for k in range(slots):
                carried = one_slot(k, carried)
        else:
            carried = lax.fori_loop(0, slots, one_slot, carried)
        squares[t] = carried[0]
        return carried[1]

    worst = lax.fori_loop(0, tiles_dev, one_tile, worst)
    worst_out[:, 0] = worst

    def send_worst(to, half):
        pltpu.make_async_remote_copy(
            src_ref=worst_out.at[to],
            dst_ref=worst_in.at[me],
            send_sem=worst_send,
            recv_sem=worst_recv,
            device_id={"blk": to, "state": half},
            device_id_type=MESH,
        ).start()

    each_peer(send_worst)
    worst_in[me] = worst_out[blk]

    def tile_peak(t, carry):
        tops[pl.ds(t, 1)] = jnp.max(squares[t].T, axis=0, keepdims=True)
        return carry

    lax.fori_loop(0, tiles_dev, tile_peak, 0)
    peak_ref[...] = jnp.sqrt((tops[0:tiles_dev] + rows[8 : 8 + tiles_dev]) * rows[16 : 16 + tiles_dev])
    table_copy.wait_send()
    pltpu.make_async_copy(pair_in.at[peers], pair_in.at[peers], pair_send).wait()
    pltpu.make_async_copy(worst_in.at[peers], worst_in.at[peers], worst_send).wait()
    pltpu.make_async_copy(worst_in.at[peers], worst_in.at[peers], worst_recv).wait()
    total = jnp.sqrt(jnp.max(worst_in[...], axis=0))
    half = pair_count // halves
    worst_ref[...] = jnp.where(is_first, total[:, :half], total[:, half:])


def write_out(peak_ref, worst_ref, peak_hbm, worst_hbm, sems):
    copies = (
        pltpu.make_async_copy(peak_ref, peak_hbm, sems.at[0]),
        pltpu.make_async_copy(worst_ref, worst_hbm, sems.at[1]),
    )
    for copy in copies:
        copy.start()
    for copy in copies:
        copy.wait()


def body(
    base_real,
    base_reactive,
    voltage,
    rating,
    monitored,
    tile_ids,
    tile_values,
    outage_ids,
    coupling,
    outage_pairs,
):
    blocks = lax.axis_size("blk")
    halves = lax.axis_size("state")
    devices = blocks * halves
    tiles_dev, slots, tile_size, _ = tile_values.shape
    pair_count = outage_pairs.shape[2]
    table_rows = base_real.shape[0] // LANES
    f32 = jnp.float32
    operands = (
        outage_pairs[0],
        coupling[0],
        outage_ids,
        base_real.reshape(table_rows, LANES),
        monitored.reshape(tiles_dev, tile_size),
        base_reactive.reshape(table_rows, LANES),
        voltage.reshape(table_rows, LANES),
        rating.reshape(table_rows, LANES),
        tile_ids,
        tile_values,
    )
    spaces = [pltpu.VMEM] * 8 + [pltpu.SMEM, pltpu.VMEM]
    shapes = (
        jax.ShapeDtypeStruct((tiles_dev, tile_size), f32),
        jax.ShapeDtypeStruct((1, pair_count // halves), f32),
    )
    vmem = pl.BlockSpec(memory_space=pltpu.VMEM)
    results = pl.pallas_call(
        functools.partial(kernel, blocks, halves),
        out_shape=shapes,
        in_specs=[pl.BlockSpec(memory_space=pltpu.HBM)] * 10,
        out_specs=(vmem, vmem),
        scratch_shapes=[space(x.shape, x.dtype) for space, x in zip(spaces, operands)]
        + [
            pltpu.VMEM((8, LANES), jnp.int32),
            pltpu.VMEM((3, table_rows, LANES), f32),
            pltpu.VMEM((3, table_rows, LANES), f32),
            pltpu.VMEM((4, pair_count), f32),
            pltpu.VMEM((devices, 4, pair_count), f32),
            pltpu.VMEM((blocks + 1, tile_size, pair_count), jnp.bfloat16),
            pltpu.VMEM((tiles_dev, 3, tile_size, pair_count), f32),
            pltpu.VMEM((LANES, LANES), f32),
            pltpu.VMEM((4, blocks, pair_count), f32),
            pltpu.VMEM((tiles_dev, tile_size, pair_count), f32),
            pltpu.VMEM((8, tile_size), f32),
            pltpu.VMEM((blocks, 1, pair_count), f32),
            pltpu.VMEM((devices, 1, pair_count), f32),
            pltpu.SemaphoreType.DMA((10,)),
            pltpu.SemaphoreType.DMA((2,)),
            pltpu.SemaphoreType.DMA(()),
            pltpu.SemaphoreType.DMA(()),
            pltpu.SemaphoreType.DMA(()),
            pltpu.SemaphoreType.DMA(()),
        ],
        compiler_params=pltpu.CompilerParams(
            collective_id=0, has_side_effects=True, vmem_limit_bytes=48 * 1024 * 1024
        ),
        name="screen",
    )(*[pltpu.with_memory_space_constraint(x, pltpu.HBM) for x in operands])
    hbm = pl.BlockSpec(memory_space=pltpu.HBM)
    peak, worst = pl.pallas_call(
        write_out,
        out_shape=shapes,
        in_specs=[vmem, vmem],
        out_specs=(hbm, hbm),
        scratch_shapes=[pltpu.SemaphoreType.DMA((2,))],
        name="write_out",
    )(*results)
    return peak.reshape(-1), worst


def solution(mesh):
    every = P(("cases", "blk", "state"))
    by_block = P(("cases", "blk"))
    return jax.shard_map(
        body,
        mesh=mesh,
        in_specs=(every,) * 7 + (by_block,) * 3,
        out_specs=(every, P(("cases", "blk"), "state")),
        check_vma=False,
    )
```

```python
import functools

import jax
import jax.numpy as jnp
from jax import lax
from jax.experimental import pallas as pl
from jax.experimental.pallas import tpu as pltpu
from jax.sharding import PartitionSpec as P

MESH = pl.DeviceIdType.MESH
LANES = 128


def take_lanes(row, lanes):
    spread = jnp.broadcast_to(row, lanes.shape)
    return jnp.take_along_axis(spread, lanes, axis=1, mode="promise_in_bounds")


def lookup(table, high, low, first_row):
    found = jnp.zeros(low.shape, table.dtype)
    for r in range(table.shape[0]):
        found = jnp.where(high == first_row + r, take_lanes(table[r : r + 1], low), found)
    return found


def kernel(
    blocks,
    halves,
    pairs_hbm,
    coup_hbm,
    out_ids_hbm,
    real_hbm,
    mon_hbm,
    react_hbm,
    volt_hbm,
    rating_hbm,
    ids_hbm,
    tiles_hbm,
    peak_ref,
    worst_ref,
    pairs_ref,
    coup_ref,
    out_ids_ref,
    real_ref,
    mon_ref,
    react_ref,
    volt_ref,
    rating_ref,
    ids_ref,
    tiles,
    index,
    table_out,
    table_in,
    pair_out,
    pair_in,
    weights,
    columns,
    rows,
    squares,
    worst_out,
    worst_in,
    load_sems,
    table_sems,
    pair_send,
    pair_recv,
    worst_send,
    worst_recv,
):
    devices = blocks * halves
    tiles_dev, slots, tile_size, _ = tiles_hbm.shape
    table_rows = real_ref.shape[0]
    blk = lax.axis_index("blk")
    state = lax.axis_index("state")
    me = state * blocks + blk

    def each_peer(step):
        if devices <= 16 and blocks & (blocks - 1) == 0:
            turns = [2**j * (1 - 2 * ((blk // 2**j) % 2)) for j in range(blocks.bit_length() - 1)]
            for apart in reversed(range(blocks)):
                to = blk + sum(turn for j, turn in enumerate(turns) if apart >> j & 1)
                step(to, 1 - state)
                if apart:
                    step(to, state)
            return
        step(blk, 1 - state)

        def one_block(i, carry):
            turned = blk + i
            to = jnp.where(turned >= blocks, turned - blocks, turned)
            step(to, state)
            step(to, 1 - state)
            return carry

        lax.fori_loop(1, blocks, one_block, 0)

    loads = [
        pltpu.make_async_copy(source, target, load_sems.at[i])
        for i, (source, target) in enumerate(
            (
                (pairs_hbm, pairs_ref),
                (coup_hbm, coup_ref),
                (out_ids_hbm, out_ids_ref),
                (real_hbm, real_ref),
                (mon_hbm, mon_ref),
                (react_hbm, react_ref),
                (volt_hbm, volt_ref),
                (rating_hbm, rating_ref),
                (ids_hbm, ids_ref),
                (tiles_hbm, tiles),
            )
        )
    ]
    for load in loads[:5]:
        load.start()
    barrier = pltpu.get_barrier_semaphore()

    def greet(to, half):
        there = {"blk": to, "state": half}
        pl.semaphore_signal(barrier, inc=1, device_id=there, device_id_type=MESH)

    each_peer(greet)
    for load in loads[5:]:
        load.start()
    for load in loads[:8]:
        load.wait()

    first, second = pairs_ref[0:1], pairs_ref[1:2]
    spot = lax.broadcasted_iota(jnp.int32, (tile_size, first.shape[1]), 0)
    at_first, at_second = spot == first, spot == second
    one, zero = jnp.float32(1.0), jnp.float32(0.0)
    picks = jnp.concatenate([jnp.where(at_second, one, zero), jnp.where(at_first, one, zero)], axis=1)
    picked = jnp.dot(coup_ref[...], picks.astype(jnp.bfloat16), preferred_element_type=jnp.float32)
    pair_count = first.shape[1]
    s_first_second = jnp.sum(jnp.where(at_first, picked[:, :pair_count], 0.0), axis=0, keepdims=True)
    s_second_first = jnp.sum(jnp.where(at_second, picked[:, pair_count:], 0.0), axis=0, keepdims=True)

    index[...] = jnp.zeros_like(index)
    index[0:tiles_dev] = mon_ref[...]
    out_ids = out_ids_ref[...]
    wide = (8, LANES)
    index[tiles_dev : tiles_dev + 1] = take_lanes(out_ids, jnp.broadcast_to(first, wide))[0:1]
    index[tiles_dev + 1 : tiles_dev + 2] = take_lanes(out_ids, jnp.broadcast_to(second, wide))[0:1]
    high, low = index[...] >> 7, index[...] & (LANES - 1)

    limit_own = volt_ref[...] * rating_ref[...]
    table_out[0] = real_ref[...]
    table_out[1] = react_ref[...]
    table_out[2] = limit_own
    own_row = state * table_rows
    real_own = lookup(real_ref[...], high, low, own_row)
    flows = real_own[tiles_dev : tiles_dev + 2].astype(jnp.bfloat16).astype(jnp.float32)
    is_first = state == 0
    pair_out[0:2] = flows
    pair_out[2:3] = jnp.where(is_first, first.astype(jnp.float32), s_first_second)
    pair_out[3:4] = jnp.where(is_first, second.astype(jnp.float32), s_second_first)

    pl.semaphore_wait(barrier, devices - 1)

    def send_pairs(to, half):
        pltpu.make_async_remote_copy(
            src_ref=pair_out,
            dst_ref=pair_in.at[me],
            send_sem=pair_send,
            recv_sem=pair_recv,
            device_id={"blk": to, "state": half},
            device_id_type=MESH,
        ).start()

    table_copy = pltpu.make_async_remote_copy(
        src_ref=table_out,
        dst_ref=table_in,
        send_sem=table_sems.at[0],
        recv_sem=table_sems.at[1],
        device_id={"state": 1 - state},
        device_id_type=MESH,
    )
    table_copy.start()
    each_peer(send_pairs)
    pair_in[me] = pair_out[...]

    react_own = lookup(react_ref[...], high, low, own_row)
    limit_mine = lookup(limit_own, high, low, own_row)
    weights[0] = jnp.zeros(weights.shape[1:], weights.dtype)
    table_copy.wait_recv()
    other_row = (1 - state) * table_rows
    mine = (high >= own_row) & (high < own_row + table_rows)
    real = jnp.where(mine, real_own, lookup(table_in[0], high, low, other_row))
    react = jnp.where(mine, react_own, lookup(table_in[1], high, low, other_row))
    limit = jnp.where(mine, limit_mine, lookup(table_in[2], high, low, other_row))
    react_sq = react * react
    rows[0:8] = real
    rows[8:16] = react_sq
    rows[16:24] = 1.0 / (limit * limit)
    rows[24:] = jnp.zeros((rows.shape[0] - 24, LANES), jnp.float32)
    upright = rows[...].T
    for t in range(tiles_dev):
        for q in range(3):
            column = upright[:, 8 * q + t : 8 * q + t + 1]
            columns[t, q] = jnp.broadcast_to(column, (tile_size, pair_count))
    loads[8].wait()
    block_of = lax.broadcasted_iota(jnp.int32, (blocks, pair_count), 0)
    worst = jnp.zeros((blocks, pair_count), jnp.float32)
    for t in range(tiles_dev):
        base = columns[t, 0]
        base_peak = jnp.max((base * base + columns[t, 1]) * columns[t, 2], axis=0, keepdims=True)
        absent = block_of >= 0
        for k in range(slots):
            absent = absent & (block_of != ids_ref[t, k])
        worst = jnp.maximum(worst, jnp.where(absent, base_peak, 0.0))
    loads[9].wait()

    peers = pl.ds(0, devices - 1)
    pltpu.make_async_copy(pair_in.at[peers], pair_in.at[peers], pair_recv).wait()
    flow_first = pair_in[0:blocks, 0] + pair_in[blocks:, 0]
    flow_second = pair_in[0:blocks, 1] + pair_in[blocks:, 1]
    first_all = pair_in[0:blocks, 2].astype(jnp.int32)
    second_all = pair_in[0:blocks, 3].astype(jnp.int32)
    s_fs, s_sf = pair_in[blocks:, 2], pair_in[blocks:, 3]
    determinant = 1.0 - s_fs * s_sf
    w_first = (flow_first + s_fs * flow_second) / determinant
    w_second = (flow_second + s_sf * flow_first) / determinant
    for b in range(blocks):
        one_row = slice(b, b + 1)
        weights[b + 1] = jnp.where(
            spot == first_all[one_row],
            w_first[one_row],
            jnp.where(spot == second_all[one_row], w_second[one_row], 0.0),
        ).astype(jnp.bfloat16)

    for t in range(tiles_dev):

        def one_slot(k, carried):
            most, worst = carried
            block = ids_ref[t, k]
            delta = jnp.dot(tiles[t, k], weights[block + 1], preferred_element_type=jnp.float32)
            post = columns[t, 0] + delta
            square = post * post
            ratio = (square + columns[t, 1]) * columns[t, 2]
            top = jnp.max(ratio, axis=0, keepdims=True)
            worst = jnp.where(block_of == block, jnp.maximum(worst, top), worst)
            return jnp.maximum(most, square), worst

        base = columns[t, 0]
        carried = (base * base, worst)
        if slots <= 4:
            for k in range(slots):
                carried = one_slot(k, carried)
        else:
            carried = lax.fori_loop(0, slots, one_slot, carried)
        most, worst = carried
        squares[t] = most
    worst_out[:, 0] = worst

    def send_worst(to, half):
        pltpu.make_async_remote_copy(
            src_ref=worst_out.at[to],
            dst_ref=worst_in.at[me],
            send_sem=worst_send,
            recv_sem=worst_recv,
            device_id={"blk": to, "state": half},
            device_id_type=MESH,
        ).start()

    each_peer(send_worst)
    worst_in[me] = worst_out[blk]
    for t in range(tiles_dev):
        most = jnp.max(squares[t].T, axis=0, keepdims=True)
        peak_ref[t : t + 1] = jnp.sqrt((most + rows[8 + t : 9 + t]) * rows[16 + t : 17 + t])

    table_copy.wait_send()
    pltpu.make_async_copy(pair_in.at[peers], pair_in.at[peers], pair_send).wait()
    pltpu.make_async_copy(worst_in.at[peers], worst_in.at[peers], worst_send).wait()
    pltpu.make_async_copy(worst_in.at[peers], worst_in.at[peers], worst_recv).wait()
    total = jnp.sqrt(jnp.max(worst_in[...], axis=0))
    half = pair_count // halves
    worst_ref[...] = jnp.where(is_first, total[:, :half], total[:, half:])


def write_out(peak_ref, worst_ref, peak_hbm, worst_hbm, sems):
    copies = (
        pltpu.make_async_copy(peak_ref, peak_hbm, sems.at[0]),
        pltpu.make_async_copy(worst_ref, worst_hbm, sems.at[1]),
    )
    for copy in copies:
        copy.start()
    for copy in copies:
        copy.wait()


def body(
    base_real,
    base_reactive,
    voltage,
    rating,
    monitored,
    tile_ids,
    tile_values,
    outage_ids,
    coupling,
    outage_pairs,
):
    blocks = lax.axis_size("blk")
    halves = lax.axis_size("state")
    devices = blocks * halves
    tiles_dev, slots, tile_size, _ = tile_values.shape
    pair_count = outage_pairs.shape[2]
    table_rows = base_real.shape[0] // LANES
    f32 = jnp.float32
    operands = (
        outage_pairs[0],
        coupling[0],
        outage_ids,
        base_real.reshape(table_rows, LANES),
        monitored.reshape(tiles_dev, tile_size),
        base_reactive.reshape(table_rows, LANES),
        voltage.reshape(table_rows, LANES),
        rating.reshape(table_rows, LANES),
        tile_ids,
        tile_values,
    )
    spaces = [pltpu.VMEM] * 8 + [pltpu.SMEM, pltpu.VMEM]
    shapes = (
        jax.ShapeDtypeStruct((tiles_dev, tile_size), f32),
        jax.ShapeDtypeStruct((1, pair_count // halves), f32),
    )
    vmem = pl.BlockSpec(memory_space=pltpu.VMEM)
    results = pl.pallas_call(
        functools.partial(kernel, blocks, halves),
        out_shape=shapes,
        in_specs=[pl.BlockSpec(memory_space=pltpu.HBM)] * 10,
        out_specs=(vmem, vmem),
        scratch_shapes=[space(x.shape, x.dtype) for space, x in zip(spaces, operands)]
        + [
            pltpu.VMEM((8, LANES), jnp.int32),
            pltpu.VMEM((3, table_rows, LANES), f32),
            pltpu.VMEM((3, table_rows, LANES), f32),
            pltpu.VMEM((4, pair_count), f32),
            pltpu.VMEM((devices, 4, pair_count), f32),
            pltpu.VMEM((blocks + 1, tile_size, pair_count), jnp.bfloat16),
            pltpu.VMEM((tiles_dev, 3, tile_size, pair_count), f32),
            pltpu.VMEM((LANES, LANES), f32),
            pltpu.VMEM((tiles_dev, tile_size, pair_count), f32),
            pltpu.VMEM((blocks, 1, pair_count), f32),
            pltpu.VMEM((devices, 1, pair_count), f32),
            pltpu.SemaphoreType.DMA((10,)),
            pltpu.SemaphoreType.DMA((2,)),
            pltpu.SemaphoreType.DMA(()),
            pltpu.SemaphoreType.DMA(()),
            pltpu.SemaphoreType.DMA(()),
            pltpu.SemaphoreType.DMA(()),
        ],
        compiler_params=pltpu.CompilerParams(
            collective_id=0, has_side_effects=True, vmem_limit_bytes=48 * 1024 * 1024
        ),
        name="screen",
    )(*[pltpu.with_memory_space_constraint(x, pltpu.HBM) for x in operands])
    hbm = pl.BlockSpec(memory_space=pltpu.HBM)
    peak, worst = pl.pallas_call(
        write_out,
        out_shape=shapes,
        in_specs=[vmem, vmem],
        out_specs=(hbm, hbm),
        scratch_shapes=[pltpu.SemaphoreType.DMA((2,))],
        compiler_params=pltpu.CompilerParams(vmem_limit_bytes=2 * 1024 * 1024),
        name="write_out",
    )(*results)
    return peak.reshape(-1), worst


def solution(mesh):
    every = P(("cases", "blk", "state"))
    by_block = P(("cases", "blk"))
    return jax.shard_map(
        body,
        mesh=mesh,
        in_specs=(every,) * 7 + (by_block,) * 3,
        out_specs=(every, P(("cases", "blk"), "state")),
        check_vma=False,
    )
```

```python
import functools

import jax
import jax.numpy as jnp
from jax import lax
from jax.experimental import pallas as pl
from jax.experimental.pallas import tpu as pltpu
from jax.sharding import PartitionSpec as P

MESH = pl.DeviceIdType.MESH
LANES = 128


def take_lanes(row, lanes):
    spread = jnp.broadcast_to(row, lanes.shape)
    return jnp.take_along_axis(spread, lanes, axis=1, mode="promise_in_bounds")


def lookup(table, high, low, first_row):
    found = jnp.zeros(low.shape, table.dtype)
    for r in range(table.shape[0]):
        found = jnp.where(high == first_row + r, take_lanes(table[r : r + 1], low), found)
    return found


def kernel(
    blocks,
    halves,
    pairs_hbm,
    coup_hbm,
    out_ids_hbm,
    real_hbm,
    mon_hbm,
    react_hbm,
    volt_hbm,
    rating_hbm,
    ids_hbm,
    tiles_hbm,
    peak_ref,
    worst_ref,
    pairs_ref,
    coup_ref,
    out_ids_ref,
    real_ref,
    mon_ref,
    react_ref,
    volt_ref,
    rating_ref,
    ids_ref,
    tiles,
    index,
    table_out,
    table_in,
    pair_out,
    pair_in,
    weights,
    columns,
    rows,
    squares,
    worst_out,
    worst_in,
    load_sems,
    table_sems,
    pair_send,
    pair_recv,
    worst_send,
    worst_recv,
):
    devices = blocks * halves
    tiles_dev, slots, tile_size, _ = tiles_hbm.shape
    table_rows = real_ref.shape[0]
    blk = lax.axis_index("blk")
    state = lax.axis_index("state")
    me = state * blocks + blk

    def each_peer(step):
        if devices <= 16 and blocks & (blocks - 1) == 0:
            turns = [2**j * (1 - 2 * ((blk // 2**j) % 2)) for j in range(blocks.bit_length() - 1)]
            for apart in reversed(range(blocks)):
                to = blk + sum(turn for j, turn in enumerate(turns) if apart >> j & 1)
                step(to, 1 - state)
                if apart:
                    step(to, state)
            return
        step(blk, 1 - state)

        def one_block(i, carry):
            turned = blk + i
            to = jnp.where(turned >= blocks, turned - blocks, turned)
            step(to, state)
            step(to, 1 - state)
            return carry

        lax.fori_loop(1, blocks, one_block, 0)

    loads = [
        pltpu.make_async_copy(source, target, load_sems.at[i])
        for i, (source, target) in enumerate(
            (
                (pairs_hbm, pairs_ref),
                (coup_hbm, coup_ref),
                (out_ids_hbm, out_ids_ref),
                (real_hbm, real_ref),
                (mon_hbm, mon_ref),
                (react_hbm, react_ref),
                (volt_hbm, volt_ref),
                (rating_hbm, rating_ref),
                (ids_hbm, ids_ref),
                (tiles_hbm, tiles),
            )
        )
    ]
    barrier = pltpu.get_barrier_semaphore()

    def greet(to, half):
        there = {"blk": to, "state": half}
        pl.semaphore_signal(barrier, inc=1, device_id=there, device_id_type=MESH)

    each_peer(greet)
    for load in loads:
        load.start()
    for load in loads[:8]:
        load.wait()

    first, second = pairs_ref[0:1], pairs_ref[1:2]
    spot = lax.broadcasted_iota(jnp.int32, (tile_size, first.shape[1]), 0)
    at_first, at_second = spot == first, spot == second
    one, zero = jnp.float32(1.0), jnp.float32(0.0)
    picks = jnp.concatenate([jnp.where(at_second, one, zero), jnp.where(at_first, one, zero)], axis=1)
    picked = jnp.dot(coup_ref[...], picks.astype(jnp.bfloat16), preferred_element_type=jnp.float32)
    pair_count = first.shape[1]
    s_first_second = jnp.sum(jnp.where(at_first, picked[:, :pair_count], 0.0), axis=0, keepdims=True)
    s_second_first = jnp.sum(jnp.where(at_second, picked[:, pair_count:], 0.0), axis=0, keepdims=True)

    index[...] = jnp.zeros_like(index)
    index[0:tiles_dev] = mon_ref[...]
    out_ids = out_ids_ref[...]
    wide = (8, LANES)
    index[tiles_dev : tiles_dev + 1] = take_lanes(out_ids, jnp.broadcast_to(first, wide))[0:1]
    index[tiles_dev + 1 : tiles_dev + 2] = take_lanes(out_ids, jnp.broadcast_to(second, wide))[0:1]
    high, low = index[...] >> 7, index[...] & (LANES - 1)

    limit_own = volt_ref[...] * rating_ref[...]
    table_out[0] = real_ref[...]
    table_out[1] = react_ref[...]
    table_out[2] = limit_own
    own_row = state * table_rows
    real_own = lookup(real_ref[...], high, low, own_row)
    flows = real_own[tiles_dev : tiles_dev + 2].astype(jnp.bfloat16).astype(jnp.float32)
    is_first = state == 0
    pair_out[0:2] = flows
    pair_out[2:3] = jnp.where(is_first, first.astype(jnp.float32), s_first_second)
    pair_out[3:4] = jnp.where(is_first, second.astype(jnp.float32), s_second_first)

    pl.semaphore_wait(barrier, devices - 1)

    def send_pairs(to, half):
        pltpu.make_async_remote_copy(
            src_ref=pair_out,
            dst_ref=pair_in.at[me],
            send_sem=pair_send,
            recv_sem=pair_recv,
            device_id={"blk": to, "state": half},
            device_id_type=MESH,
        ).start()

    table_copy = pltpu.make_async_remote_copy(
        src_ref=table_out,
        dst_ref=table_in,
        send_sem=table_sems.at[0],
        recv_sem=table_sems.at[1],
        device_id={"state": 1 - state},
        device_id_type=MESH,
    )
    table_copy.start()
    each_peer(send_pairs)
    pair_in[me] = pair_out[...]

    react_own = lookup(react_ref[...], high, low, own_row)
    limit_mine = lookup(limit_own, high, low, own_row)
    weights[0] = jnp.zeros(weights.shape[1:], weights.dtype)
    table_copy.wait_recv()
    other_row = (1 - state) * table_rows
    mine = (high >= own_row) & (high < own_row + table_rows)
    real = jnp.where(mine, real_own, lookup(table_in[0], high, low, other_row))
    react = jnp.where(mine, react_own, lookup(table_in[1], high, low, other_row))
    limit = jnp.where(mine, limit_mine, lookup(table_in[2], high, low, other_row))
    react_sq = react * react
    rows[0:8] = real
    rows[8:16] = react_sq
    rows[16:24] = 1.0 / (limit * limit)
    rows[24:] = jnp.zeros((rows.shape[0] - 24, LANES), jnp.float32)
    upright = rows[...].T
    for t in range(tiles_dev):
        for q in range(3):
            column = upright[:, 8 * q + t : 8 * q + t + 1]
            columns[t, q] = jnp.broadcast_to(column, (tile_size, pair_count))
    loads[8].wait()
    block_of = lax.broadcasted_iota(jnp.int32, (blocks, pair_count), 0)
    worst = jnp.zeros((blocks, pair_count), jnp.float32)
    for t in range(tiles_dev):
        base = columns[t, 0]
        base_peak = jnp.max((base * base + columns[t, 1]) * columns[t, 2], axis=0, keepdims=True)
        absent = block_of >= 0
        for k in range(slots):
            absent = absent & (block_of != ids_ref[t, k])
        worst = jnp.maximum(worst, jnp.where(absent, base_peak, 0.0))
    loads[9].wait()

    peers = pl.ds(0, devices - 1)
    pltpu.make_async_copy(pair_in.at[peers], pair_in.at[peers], pair_recv).wait()
    flow_first = pair_in[0:blocks, 0] + pair_in[blocks:, 0]
    flow_second = pair_in[0:blocks, 1] + pair_in[blocks:, 1]
    first_all, second_all = pair_in[0:blocks, 2], pair_in[0:blocks, 3]
    places = spot.astype(jnp.float32).astype(jnp.bfloat16).reshape(tile_size // 16, 16, pair_count)
    s_fs, s_sf = pair_in[blocks:, 2], pair_in[blocks:, 3]
    determinant = 1.0 - s_fs * s_sf
    w_first = (flow_first + s_fs * flow_second) / determinant
    w_second = (flow_second + s_sf * flow_first) / determinant
    packed = (16, pair_count)

    def spread(rows_all, b):
        return jnp.broadcast_to(rows_all[b : b + 1], packed).astype(jnp.bfloat16)[None]

    none = jnp.zeros((1, *packed), jnp.bfloat16)
    for b in range(blocks):
        weights[b + 1] = jnp.where(
            places == spread(first_all, b),
            spread(w_first, b),
            jnp.where(places == spread(second_all, b), spread(w_second, b), none),
        ).reshape(tile_size, pair_count)

    for t in range(tiles_dev):

        def one_slot(k, carried):
            most, worst = carried
            block = ids_ref[t, k]
            delta = jnp.dot(tiles[t, k], weights[block + 1], preferred_element_type=jnp.float32)
            post = columns[t, 0] + delta
            square = post * post
            ratio = (square + columns[t, 1]) * columns[t, 2]
            top = jnp.max(ratio, axis=0, keepdims=True)
            worst = jnp.where(block_of == block, jnp.maximum(worst, top), worst)
            return jnp.maximum(most, square), worst

        base = columns[t, 0]
        carried = (base * base, worst)
        if slots <= 4:
            for k in range(slots):
                carried = one_slot(k, carried)
        else:
            carried = lax.fori_loop(0, slots, one_slot, carried)
        most, worst = carried
        squares[t] = most
    worst_out[:, 0] = worst

    def send_worst(to, half):
        pltpu.make_async_remote_copy(
            src_ref=worst_out.at[to],
            dst_ref=worst_in.at[me],
            send_sem=worst_send,
            recv_sem=worst_recv,
            device_id={"blk": to, "state": half},
            device_id_type=MESH,
        ).start()

    each_peer(send_worst)
    worst_in[me] = worst_out[blk]
    for t in range(tiles_dev):
        most = jnp.max(squares[t].T, axis=0, keepdims=True)
        peak_ref[t : t + 1] = jnp.sqrt((most + rows[8 + t : 9 + t]) * rows[16 + t : 17 + t])

    table_copy.wait_send()
    pltpu.make_async_copy(pair_in.at[peers], pair_in.at[peers], pair_send).wait()
    pltpu.make_async_copy(worst_in.at[peers], worst_in.at[peers], worst_send).wait()
    pltpu.make_async_copy(worst_in.at[peers], worst_in.at[peers], worst_recv).wait()
    total = jnp.sqrt(jnp.max(worst_in[...], axis=0))
    half = pair_count // halves
    worst_ref[...] = jnp.where(is_first, total[:, :half], total[:, half:])


def write_out(peak_ref, worst_ref, peak_hbm, worst_hbm, sems):
    copies = (
        pltpu.make_async_copy(peak_ref, peak_hbm, sems.at[0]),
        pltpu.make_async_copy(worst_ref, worst_hbm, sems.at[1]),
    )
    for copy in copies:
        copy.start()
    for copy in copies:
        copy.wait()


def body(
    base_real,
    base_reactive,
    voltage,
    rating,
    monitored,
    tile_ids,
    tile_values,
    outage_ids,
    coupling,
    outage_pairs,
):
    blocks = lax.axis_size("blk")
    halves = lax.axis_size("state")
    devices = blocks * halves
    tiles_dev, slots, tile_size, _ = tile_values.shape
    pair_count = outage_pairs.shape[2]
    table_rows = base_real.shape[0] // LANES
    f32 = jnp.float32
    operands = (
        outage_pairs[0],
        coupling[0],
        outage_ids,
        base_real.reshape(table_rows, LANES),
        monitored.reshape(tiles_dev, tile_size),
        base_reactive.reshape(table_rows, LANES),
        voltage.reshape(table_rows, LANES),
        rating.reshape(table_rows, LANES),
        tile_ids,
        tile_values,
    )
    spaces = [pltpu.VMEM] * 8 + [pltpu.SMEM, pltpu.VMEM]
    shapes = (
        jax.ShapeDtypeStruct((tiles_dev, tile_size), f32),
        jax.ShapeDtypeStruct((1, pair_count // halves), f32),
    )
    vmem = pl.BlockSpec(memory_space=pltpu.VMEM)
    results = pl.pallas_call(
        functools.partial(kernel, blocks, halves),
        out_shape=shapes,
        in_specs=[pl.BlockSpec(memory_space=pltpu.HBM)] * 10,
        out_specs=(vmem, vmem),
        scratch_shapes=[space(x.shape, x.dtype) for space, x in zip(spaces, operands)]
        + [
            pltpu.VMEM((8, LANES), jnp.int32),
            pltpu.VMEM((3, table_rows, LANES), f32),
            pltpu.VMEM((3, table_rows, LANES), f32),
            pltpu.VMEM((4, pair_count), f32),
            pltpu.VMEM((devices, 4, pair_count), f32),
            pltpu.VMEM((blocks + 1, tile_size, pair_count), jnp.bfloat16),
            pltpu.VMEM((tiles_dev, 3, tile_size, pair_count), f32),
            pltpu.VMEM((LANES, LANES), f32),
            pltpu.VMEM((tiles_dev, tile_size, pair_count), f32),
            pltpu.VMEM((blocks, 1, pair_count), f32),
            pltpu.VMEM((devices, 1, pair_count), f32),
            pltpu.SemaphoreType.DMA((10,)),
            pltpu.SemaphoreType.DMA((2,)),
            pltpu.SemaphoreType.DMA(()),
            pltpu.SemaphoreType.DMA(()),
            pltpu.SemaphoreType.DMA(()),
            pltpu.SemaphoreType.DMA(()),
        ],
        compiler_params=pltpu.CompilerParams(
            collective_id=0, has_side_effects=True, vmem_limit_bytes=48 * 1024 * 1024
        ),
        name="screen",
    )(*[pltpu.with_memory_space_constraint(x, pltpu.HBM) for x in operands])
    hbm = pl.BlockSpec(memory_space=pltpu.HBM)
    peak, worst = pl.pallas_call(
        write_out,
        out_shape=shapes,
        in_specs=[vmem, vmem],
        out_specs=(hbm, hbm),
        scratch_shapes=[pltpu.SemaphoreType.DMA((2,))],
        compiler_params=pltpu.CompilerParams(vmem_limit_bytes=2 * 1024 * 1024),
        name="write_out",
    )(*results)
    return peak.reshape(-1), worst


def solution(mesh):
    every = P(("cases", "blk", "state"))
    by_block = P(("cases", "blk"))
    return jax.shard_map(
        body,
        mesh=mesh,
        in_specs=(every,) * 7 + (by_block,) * 3,
        out_specs=(every, P(("cases", "blk"), "state")),
        check_vma=False,
    )
```

```python
import functools

import jax
import jax.numpy as jnp
from jax import lax
from jax.experimental import pallas as pl
from jax.experimental.pallas import tpu as pltpu
from jax.sharding import PartitionSpec as P

MESH = pl.DeviceIdType.MESH
LANES = 128


def take_lanes(row, lanes):
    spread = jnp.broadcast_to(row, lanes.shape)
    return jnp.take_along_axis(spread, lanes, axis=1, mode="promise_in_bounds")


def lookup(table, high, low, first_row):
    found = jnp.zeros(low.shape, table.dtype)
    for r in range(table.shape[0]):
        found = jnp.where(high == first_row + r, take_lanes(table[r : r + 1], low), found)
    return found


def kernel(
    blocks,
    halves,
    pairs_hbm,
    coup_hbm,
    out_ids_hbm,
    real_hbm,
    mon_hbm,
    react_hbm,
    volt_hbm,
    rating_hbm,
    ids_hbm,
    tiles_hbm,
    peak_ref,
    worst_ref,
    pairs_ref,
    coup_ref,
    out_ids_ref,
    real_ref,
    mon_ref,
    react_ref,
    volt_ref,
    rating_ref,
    ids_ref,
    tiles,
    index,
    table_out,
    table_in,
    pair_out,
    pair_in,
    weights,
    columns,
    rows,
    squares,
    worst_out,
    worst_in,
    load_sems,
    table_sems,
    pair_send,
    pair_recv,
    worst_send,
    worst_recv,
):
    devices = blocks * halves
    tiles_dev, slots, tile_size, _ = tiles_hbm.shape
    table_rows = real_ref.shape[0]
    blk = lax.axis_index("blk")
    state = lax.axis_index("state")
    me = state * blocks + blk

    def each_peer(step):
        if devices <= 16 and blocks & (blocks - 1) == 0:
            turns = [2**j * (1 - 2 * ((blk // 2**j) % 2)) for j in range(blocks.bit_length() - 1)]
            for apart in reversed(range(blocks)):
                to = blk + sum(turn for j, turn in enumerate(turns) if apart >> j & 1)
                step(to, 1 - state)
                if apart:
                    step(to, state)
            return
        step(blk, 1 - state)

        def one_block(i, carry):
            turned = blk + i
            to = jnp.where(turned >= blocks, turned - blocks, turned)
            step(to, state)
            step(to, 1 - state)
            return carry

        lax.fori_loop(1, blocks, one_block, 0)

    loads = [
        pltpu.make_async_copy(source, target, load_sems.at[i])
        for i, (source, target) in enumerate(
            (
                (pairs_hbm, pairs_ref),
                (coup_hbm, coup_ref),
                (out_ids_hbm, out_ids_ref),
                (real_hbm, real_ref),
                (mon_hbm, mon_ref),
                (react_hbm, react_ref),
                (volt_hbm, volt_ref),
                (rating_hbm, rating_ref),
                (ids_hbm, ids_ref),
                (tiles_hbm, tiles),
            )
        )
    ]
    barrier = pltpu.get_barrier_semaphore()

    def greet(to, half):
        there = {"blk": to, "state": half}
        pl.semaphore_signal(barrier, inc=1, device_id=there, device_id_type=MESH)

    each_peer(greet)
    for load in loads:
        load.start()
    for load in loads[:8]:
        load.wait()

    first, second = pairs_ref[0:1], pairs_ref[1:2]
    spot = lax.broadcasted_iota(jnp.int32, (tile_size, first.shape[1]), 0)
    at_first, at_second = spot == first, spot == second
    one, zero = jnp.float32(1.0), jnp.float32(0.0)
    picks = jnp.concatenate([jnp.where(at_second, one, zero), jnp.where(at_first, one, zero)], axis=1)
    picked = jnp.dot(coup_ref[...], picks.astype(jnp.bfloat16), preferred_element_type=jnp.float32)
    pair_count = first.shape[1]
    s_first_second = jnp.sum(jnp.where(at_first, picked[:, :pair_count], 0.0), axis=0, keepdims=True)
    s_second_first = jnp.sum(jnp.where(at_second, picked[:, pair_count:], 0.0), axis=0, keepdims=True)

    index[...] = jnp.zeros_like(index)
    index[0:tiles_dev] = mon_ref[...]
    out_ids = out_ids_ref[...]
    wide = (8, LANES)
    index[tiles_dev : tiles_dev + 1] = take_lanes(out_ids, jnp.broadcast_to(first, wide))[0:1]
    index[tiles_dev + 1 : tiles_dev + 2] = take_lanes(out_ids, jnp.broadcast_to(second, wide))[0:1]
    high, low = index[...] >> 7, index[...] & (LANES - 1)

    limit_own = volt_ref[...] * rating_ref[...]
    table_out[0] = real_ref[...]
    table_out[1] = react_ref[...]
    table_out[2] = limit_own
    own_row = state * table_rows
    real_own = lookup(real_ref[...], high, low, own_row)
    flows = real_own[tiles_dev : tiles_dev + 2].astype(jnp.bfloat16).astype(jnp.float32)
    is_first = state == 0
    pair_out[0] = flows[0:1]
    pair_out[1] = flows[1:2]
    pair_out[2] = jnp.where(is_first, first.astype(jnp.float32), s_first_second)
    pair_out[3] = jnp.where(is_first, second.astype(jnp.float32), s_second_first)

    pl.semaphore_wait(barrier, devices - 1)

    def send_pairs(to, half):
        pltpu.make_async_remote_copy(
            src_ref=pair_out,
            dst_ref=pair_in.at[:, pl.ds(me, 1)],
            send_sem=pair_send,
            recv_sem=pair_recv,
            device_id={"blk": to, "state": half},
            device_id_type=MESH,
        ).start()

    table_copy = pltpu.make_async_remote_copy(
        src_ref=table_out,
        dst_ref=table_in,
        send_sem=table_sems.at[0],
        recv_sem=table_sems.at[1],
        device_id={"state": 1 - state},
        device_id_type=MESH,
    )
    table_copy.start()
    each_peer(send_pairs)
    pair_in[:, pl.ds(me, 1)] = pair_out[...]

    react_own = lookup(react_ref[...], high, low, own_row)
    limit_mine = lookup(limit_own, high, low, own_row)
    weights[0] = jnp.zeros(weights.shape[1:], weights.dtype)
    table_copy.wait_recv()
    other_row = (1 - state) * table_rows
    mine = (high >= own_row) & (high < own_row + table_rows)
    real = jnp.where(mine, real_own, lookup(table_in[0], high, low, other_row))
    react = jnp.where(mine, react_own, lookup(table_in[1], high, low, other_row))
    limit = jnp.where(mine, limit_mine, lookup(table_in[2], high, low, other_row))
    react_sq = react * react
    rows[0:8] = real
    rows[8:16] = react_sq
    rows[16:24] = 1.0 / (limit * limit)
    rows[24:] = jnp.zeros((rows.shape[0] - 24, LANES), jnp.float32)
    upright = rows[...].T
    for t in range(tiles_dev):
        for q in range(3):
            column = upright[:, 8 * q + t : 8 * q + t + 1]
            columns[t, q] = jnp.broadcast_to(column, (tile_size, pair_count))
    loads[8].wait()
    block_of = lax.broadcasted_iota(jnp.int32, (blocks, pair_count), 0)
    worst = jnp.zeros((blocks, pair_count), jnp.float32)
    for t in range(tiles_dev):
        base = columns[t, 0]
        base_peak = jnp.max((base * base + columns[t, 1]) * columns[t, 2], axis=0, keepdims=True)
        absent = block_of >= 0
        for k in range(slots):
            absent = absent & (block_of != ids_ref[t, k])
        worst = jnp.maximum(worst, jnp.where(absent, base_peak, 0.0))
    loads[9].wait()

    peers = pl.ds(0, devices - 1)
    pltpu.make_async_copy(pair_in.at[:, peers], pair_in.at[:, peers], pair_recv).wait()
    flow_first = pair_in[0, 0:blocks] + pair_in[0, blocks:]
    flow_second = pair_in[1, 0:blocks] + pair_in[1, blocks:]
    first_all, second_all = pair_in[2, 0:blocks], pair_in[3, 0:blocks]
    places = spot.astype(jnp.float32).astype(jnp.bfloat16).reshape(tile_size // 16, 16, pair_count)
    s_fs, s_sf = pair_in[2, blocks:], pair_in[3, blocks:]
    determinant = 1.0 - s_fs * s_sf
    w_first = (flow_first + s_fs * flow_second) / determinant
    w_second = (flow_second + s_sf * flow_first) / determinant
    packed = (16, pair_count)

    def spread(rows_all, b):
        return jnp.broadcast_to(rows_all[b : b + 1], packed).astype(jnp.bfloat16)[None]

    none = jnp.zeros((1, *packed), jnp.bfloat16)
    for b in range(blocks):
        weights[b + 1] = jnp.where(
            places == spread(first_all, b),
            spread(w_first, b),
            jnp.where(places == spread(second_all, b), spread(w_second, b), none),
        ).reshape(tile_size, pair_count)

    for t in range(tiles_dev):

        def one_slot(k, carried):
            most, worst = carried
            block = ids_ref[t, k]
            delta = jnp.dot(tiles[t, k], weights[block + 1], preferred_element_type=jnp.float32)
            post = columns[t, 0] + delta
            square = post * post
            ratio = (square + columns[t, 1]) * columns[t, 2]
            top = jnp.max(ratio, axis=0, keepdims=True)
            worst = jnp.where(block_of == block, jnp.maximum(worst, top), worst)
            return jnp.maximum(most, square), worst

        base = columns[t, 0]
        carried = (base * base, worst)
        if slots <= 4:
            for k in range(slots):
                carried = one_slot(k, carried)
        else:
            carried = lax.fori_loop(0, slots, one_slot, carried)
        most, worst = carried
        squares[t] = most
    worst_out[...] = worst

    def send_worst(to, half):
        pltpu.make_async_remote_copy(
            src_ref=worst_out.at[pl.ds(to, 1)],
            dst_ref=worst_in.at[pl.ds(me, 1)],
            send_sem=worst_send,
            recv_sem=worst_recv,
            device_id={"blk": to, "state": half},
            device_id_type=MESH,
        ).start()

    each_peer(send_worst)
    worst_in[pl.ds(me, 1)] = worst_out[pl.ds(blk, 1)]
    for t in range(tiles_dev):
        most = jnp.max(squares[t].T, axis=0, keepdims=True)
        peak_ref[t : t + 1] = jnp.sqrt((most + rows[8 + t : 9 + t]) * rows[16 + t : 17 + t])

    table_copy.wait_send()
    pltpu.make_async_copy(pair_in.at[:, peers], pair_in.at[:, peers], pair_send).wait()
    pltpu.make_async_copy(worst_in.at[peers], worst_in.at[peers], worst_send).wait()
    pltpu.make_async_copy(worst_in.at[peers], worst_in.at[peers], worst_recv).wait()
    total = jnp.sqrt(jnp.max(worst_in[...], axis=0, keepdims=True))
    half = pair_count // halves
    worst_ref[...] = jnp.where(is_first, total[:, :half], total[:, half:])


def write_out(peak_ref, worst_ref, peak_hbm, worst_hbm, sems):
    copies = (
        pltpu.make_async_copy(peak_ref, peak_hbm, sems.at[0]),
        pltpu.make_async_copy(worst_ref, worst_hbm, sems.at[1]),
    )
    for copy in copies:
        copy.start()
    for copy in copies:
        copy.wait()


def body(
    base_real,
    base_reactive,
    voltage,
    rating,
    monitored,
    tile_ids,
    tile_values,
    outage_ids,
    coupling,
    outage_pairs,
):
    blocks = lax.axis_size("blk")
    halves = lax.axis_size("state")
    devices = blocks * halves
    tiles_dev, slots, tile_size, _ = tile_values.shape
    pair_count = outage_pairs.shape[2]
    table_rows = base_real.shape[0] // LANES
    f32 = jnp.float32
    operands = (
        outage_pairs[0],
        coupling[0],
        outage_ids,
        base_real.reshape(table_rows, LANES),
        monitored.reshape(tiles_dev, tile_size),
        base_reactive.reshape(table_rows, LANES),
        voltage.reshape(table_rows, LANES),
        rating.reshape(table_rows, LANES),
        tile_ids,
        tile_values,
    )
    spaces = [pltpu.VMEM] * 8 + [pltpu.SMEM, pltpu.VMEM]
    shapes = (
        jax.ShapeDtypeStruct((tiles_dev, tile_size), f32),
        jax.ShapeDtypeStruct((1, pair_count // halves), f32),
    )
    vmem = pl.BlockSpec(memory_space=pltpu.VMEM)
    results = pl.pallas_call(
        functools.partial(kernel, blocks, halves),
        out_shape=shapes,
        in_specs=[pl.BlockSpec(memory_space=pltpu.HBM)] * 10,
        out_specs=(vmem, vmem),
        scratch_shapes=[space(x.shape, x.dtype) for space, x in zip(spaces, operands)]
        + [
            pltpu.VMEM((8, LANES), jnp.int32),
            pltpu.VMEM((3, table_rows, LANES), f32),
            pltpu.VMEM((3, table_rows, LANES), f32),
            pltpu.VMEM((4, 1, pair_count), f32),
            pltpu.VMEM((4, devices, pair_count), f32),
            pltpu.VMEM((blocks + 1, tile_size, pair_count), jnp.bfloat16),
            pltpu.VMEM((tiles_dev, 3, tile_size, pair_count), f32),
            pltpu.VMEM((LANES, LANES), f32),
            pltpu.VMEM((tiles_dev, tile_size, pair_count), f32),
            pltpu.VMEM((blocks, pair_count), f32),
            pltpu.VMEM((devices, pair_count), f32),
            pltpu.SemaphoreType.DMA((10,)),
            pltpu.SemaphoreType.DMA((2,)),
            pltpu.SemaphoreType.DMA(()),
            pltpu.SemaphoreType.DMA(()),
            pltpu.SemaphoreType.DMA(()),
            pltpu.SemaphoreType.DMA(()),
        ],
        compiler_params=pltpu.CompilerParams(
            collective_id=0, has_side_effects=True, vmem_limit_bytes=48 * 1024 * 1024
        ),
        name="screen",
    )(*[pltpu.with_memory_space_constraint(x, pltpu.HBM) for x in operands])
    hbm = pl.BlockSpec(memory_space=pltpu.HBM)
    peak, worst = pl.pallas_call(
        write_out,
        out_shape=shapes,
        in_specs=[vmem, vmem],
        out_specs=(hbm, hbm),
        scratch_shapes=[pltpu.SemaphoreType.DMA((2,))],
        compiler_params=pltpu.CompilerParams(vmem_limit_bytes=2 * 1024 * 1024),
        name="write_out",
    )(*results)
    return peak.reshape(-1), worst


def solution(mesh):
    every = P(("cases", "blk", "state"))
    by_block = P(("cases", "blk"))
    return jax.shard_map(
        body,
        mesh=mesh,
        in_specs=(every,) * 7 + (by_block,) * 3,
        out_specs=(every, P(("cases", "blk"), "state")),
        check_vma=False,
    )
```

```python
import functools

import jax
import jax.numpy as jnp
from jax import lax
from jax.experimental import pallas as pl
from jax.experimental.pallas import tpu as pltpu
from jax.sharding import PartitionSpec as P

MESH = pl.DeviceIdType.MESH
LANES = 128


def take_lanes(row, lanes):
    spread = jnp.broadcast_to(row, lanes.shape)
    return jnp.take_along_axis(spread, lanes, axis=1, mode="promise_in_bounds")


def lookup(table, high, low, first_row):
    found = jnp.zeros(low.shape, table.dtype)
    for r in range(table.shape[0]):
        found = jnp.where(high == first_row + r, take_lanes(table[r : r + 1], low), found)
    return found


def kernel(
    blocks,
    halves,
    pairs_hbm,
    coup_hbm,
    out_ids_hbm,
    real_hbm,
    mon_hbm,
    react_hbm,
    volt_hbm,
    rating_hbm,
    ids_hbm,
    tiles_hbm,
    peak_ref,
    worst_ref,
    pairs_ref,
    coup_ref,
    out_ids_ref,
    real_ref,
    mon_ref,
    react_ref,
    volt_ref,
    rating_ref,
    ids_ref,
    tiles,
    index,
    table_out,
    table_in,
    pair_out,
    pair_in,
    weights,
    columns,
    rows,
    squares,
    worst_out,
    worst_in,
    load_sems,
    table_sems,
    pair_send,
    pair_recv,
    worst_send,
    worst_recv,
):
    devices = blocks * halves
    tiles_dev, slots, tile_size, _ = tiles_hbm.shape
    table_rows = real_ref.shape[0]
    blk = lax.axis_index("blk")
    state = lax.axis_index("state")
    me = state * blocks + blk

    def each_peer(step):
        if devices <= 16 and blocks & (blocks - 1) == 0:
            turns = [2**j * (1 - 2 * ((blk // 2**j) % 2)) for j in range(blocks.bit_length() - 1)]
            for apart in reversed(range(blocks)):
                to = blk + sum(turn for j, turn in enumerate(turns) if apart >> j & 1)
                step(to, 1 - state)
                if apart:
                    step(to, state)
            return
        step(blk, 1 - state)

        def one_block(i, carry):
            turned = blk + i
            to = jnp.where(turned >= blocks, turned - blocks, turned)
            step(to, state)
            step(to, 1 - state)
            return carry

        lax.fori_loop(1, blocks, one_block, 0)

    loads = [
        pltpu.make_async_copy(source, target, load_sems.at[i])
        for i, (source, target) in enumerate(
            (
                (pairs_hbm, pairs_ref),
                (coup_hbm, coup_ref),
                (out_ids_hbm, out_ids_ref),
                (real_hbm, real_ref),
                (mon_hbm, mon_ref),
                (react_hbm, react_ref),
                (volt_hbm, volt_ref),
                (rating_hbm, rating_ref),
                (ids_hbm, ids_ref),
                (tiles_hbm, tiles),
            )
        )
    ]
    for load in loads[:5]:
        load.start()
    barrier = pltpu.get_barrier_semaphore()

    def greet(to, half):
        there = {"blk": to, "state": half}
        pl.semaphore_signal(barrier, inc=1, device_id=there, device_id_type=MESH)

    each_peer(greet)
    for load in loads[5:]:
        load.start()
    for load in loads[:5]:
        load.wait()

    first, second = pairs_ref[0:1], pairs_ref[1:2]
    spot = lax.broadcasted_iota(jnp.int32, (tile_size, first.shape[1]), 0)
    at_first, at_second = spot == first, spot == second
    one, zero = jnp.float32(1.0), jnp.float32(0.0)
    picks = jnp.concatenate([jnp.where(at_second, one, zero), jnp.where(at_first, one, zero)], axis=1)
    picked = jnp.dot(coup_ref[...], picks.astype(jnp.bfloat16), preferred_element_type=jnp.float32)
    pair_count = first.shape[1]
    s_first_second = jnp.sum(jnp.where(at_first, picked[:, :pair_count], 0.0), axis=0, keepdims=True)
    s_second_first = jnp.sum(jnp.where(at_second, picked[:, pair_count:], 0.0), axis=0, keepdims=True)

    index[...] = jnp.zeros_like(index)
    index[0:tiles_dev] = mon_ref[...]
    out_ids = out_ids_ref[...]
    wide = (8, LANES)
    index[tiles_dev : tiles_dev + 1] = take_lanes(out_ids, jnp.broadcast_to(first, wide))[0:1]
    index[tiles_dev + 1 : tiles_dev + 2] = take_lanes(out_ids, jnp.broadcast_to(second, wide))[0:1]
    high, low = index[...] >> 7, index[...] & (LANES - 1)

    own_row = state * table_rows
    real_own = lookup(real_ref[...], high, low, own_row)
    flows = real_own[tiles_dev : tiles_dev + 2].astype(jnp.bfloat16).astype(jnp.float32)
    is_first = state == 0
    pair_out[0] = flows[0:1]
    pair_out[1] = flows[1:2]
    pair_out[2] = jnp.where(is_first, first.astype(jnp.float32), s_first_second)
    pair_out[3] = jnp.where(is_first, second.astype(jnp.float32), s_second_first)

    pl.semaphore_wait(barrier, devices - 1)

    def send_pairs(to, half):
        pltpu.make_async_remote_copy(
            src_ref=pair_out,
            dst_ref=pair_in.at[:, pl.ds(me, 1)],
            send_sem=pair_send,
            recv_sem=pair_recv,
            device_id={"blk": to, "state": half},
            device_id_type=MESH,
        ).start()

    table_copy = pltpu.make_async_remote_copy(
        src_ref=table_out,
        dst_ref=table_in,
        send_sem=table_sems.at[0],
        recv_sem=table_sems.at[1],
        device_id={"state": 1 - state},
        device_id_type=MESH,
    )
    each_peer(send_pairs)
    for load in loads[5:8]:
        load.wait()
    limit_own = volt_ref[...] * rating_ref[...]
    table_out[0] = real_ref[...]
    table_out[1] = react_ref[...]
    table_out[2] = limit_own
    table_copy.start()
    pair_in[:, pl.ds(me, 1)] = pair_out[...]

    react_own = lookup(react_ref[...], high, low, own_row)
    limit_mine = lookup(limit_own, high, low, own_row)
    weights[0] = jnp.zeros(weights.shape[1:], weights.dtype)
    table_copy.wait_recv()
    other_row = (1 - state) * table_rows
    mine = (high >= own_row) & (high < own_row + table_rows)
    real = jnp.where(mine, real_own, lookup(table_in[0], high, low, other_row))
    react = jnp.where(mine, react_own, lookup(table_in[1], high, low, other_row))
    limit = jnp.where(mine, limit_mine, lookup(table_in[2], high, low, other_row))
    react_sq = react * react
    rows[0:8] = real
    rows[8:16] = react_sq
    rows[16:24] = 1.0 / (limit * limit)
    rows[24:] = jnp.zeros((rows.shape[0] - 24, LANES), jnp.float32)
    upright = rows[...].T
    for t in range(tiles_dev):
        for q in range(3):
            column = upright[:, 8 * q + t : 8 * q + t + 1]
            columns[t, q] = jnp.broadcast_to(column, (tile_size, pair_count))
    loads[8].wait()
    block_of = lax.broadcasted_iota(jnp.int32, (blocks, pair_count), 0)
    worst = jnp.zeros((blocks, pair_count), jnp.float32)
    for t in range(tiles_dev):
        base = columns[t, 0]
        base_peak = jnp.max((base * base + columns[t, 1]) * columns[t, 2], axis=0, keepdims=True)
        absent = block_of >= 0
        for k in range(slots):
            absent = absent & (block_of != ids_ref[t, k])
        worst = jnp.maximum(worst, jnp.where(absent, base_peak, 0.0))
    loads[9].wait()

    peers = pl.ds(0, devices - 1)
    pltpu.make_async_copy(pair_in.at[:, peers], pair_in.at[:, peers], pair_recv).wait()
    flow_first = pair_in[0, 0:blocks] + pair_in[0, blocks:]
    flow_second = pair_in[1, 0:blocks] + pair_in[1, blocks:]
    first_all, second_all = pair_in[2, 0:blocks], pair_in[3, 0:blocks]
    places = spot.astype(jnp.float32).astype(jnp.bfloat16).reshape(tile_size // 16, 16, pair_count)
    s_fs, s_sf = pair_in[2, blocks:], pair_in[3, blocks:]
    determinant = 1.0 - s_fs * s_sf
    w_first = (flow_first + s_fs * flow_second) / determinant
    w_second = (flow_second + s_sf * flow_first) / determinant
    packed = (16, pair_count)

    def spread(rows_all, b):
        return jnp.broadcast_to(rows_all[b : b + 1], packed).astype(jnp.bfloat16)[None]

    none = jnp.zeros((1, *packed), jnp.bfloat16)
    for b in range(blocks):
        weights[b + 1] = jnp.where(
            places == spread(first_all, b),
            spread(w_first, b),
            jnp.where(places == spread(second_all, b), spread(w_second, b), none),
        ).reshape(tile_size, pair_count)

    for t in range(tiles_dev):

        def absorb(k, delta, most, worst):
            post = columns[t, 0] + delta
            square = post * post
            ratio = (square + columns[t, 1]) * columns[t, 2]
            top = jnp.max(ratio, axis=0, keepdims=True)
            worst = jnp.where(block_of == ids_ref[t, k], jnp.maximum(worst, top), worst)
            return jnp.maximum(most, square), worst

        def two_slots(i, carried):
            k = 2 * i
            first_w, second_w = weights[ids_ref[t, k] + 1], weights[ids_ref[t, k + 1] + 1]
            blank = jnp.zeros_like(first_w)
            both = jnp.concatenate(
                [
                    jnp.concatenate([first_w, blank], axis=1),
                    jnp.concatenate([blank, second_w], axis=1),
                ],
                axis=0,
            )
            held = jnp.concatenate([tiles[t, k], tiles[t, k + 1]], axis=1)
            delta = jnp.dot(held, both, preferred_element_type=jnp.float32)
            carried = absorb(k, delta[:, :pair_count], *carried)
            return absorb(k + 1, delta[:, pair_count:], *carried)

        def one_slot(k, carried):
            weight = weights[ids_ref[t, k] + 1]
            delta = jnp.dot(tiles[t, k], weight, preferred_element_type=jnp.float32)
            return absorb(k, delta, *carried)

        base = columns[t, 0]
        carried = (base * base, worst)
        if slots <= 4:
            for i in range(slots // 2):
                carried = two_slots(i, carried)
        else:
            carried = lax.fori_loop(0, slots // 2, two_slots, carried)
        if slots % 2:
            carried = one_slot(slots - 1, carried)
        most, worst = carried
        squares[t] = most
    worst_out[...] = worst

    def send_worst(to, half):
        pltpu.make_async_remote_copy(
            src_ref=worst_out.at[pl.ds(to, 1)],
            dst_ref=worst_in.at[pl.ds(me, 1)],
            send_sem=worst_send,
            recv_sem=worst_recv,
            device_id={"blk": to, "state": half},
            device_id_type=MESH,
        ).start()

    each_peer(send_worst)
    worst_in[pl.ds(me, 1)] = worst_out[pl.ds(blk, 1)]
    for t in range(tiles_dev):
        most = jnp.max(squares[t].T, axis=0, keepdims=True)
        peak_ref[t : t + 1] = jnp.sqrt((most + rows[8 + t : 9 + t]) * rows[16 + t : 17 + t])

    table_copy.wait_send()
    pltpu.make_async_copy(pair_in.at[:, peers], pair_in.at[:, peers], pair_send).wait()
    pltpu.make_async_copy(worst_in.at[peers], worst_in.at[peers], worst_send).wait()
    pltpu.make_async_copy(worst_in.at[peers], worst_in.at[peers], worst_recv).wait()
    total = jnp.sqrt(jnp.max(worst_in[...], axis=0, keepdims=True))
    half = pair_count // halves
    worst_ref[...] = jnp.where(is_first, total[:, :half], total[:, half:])


def write_out(peak_ref, worst_ref, peak_hbm, worst_hbm, sems):
    copies = (
        pltpu.make_async_copy(peak_ref, peak_hbm, sems.at[0]),
        pltpu.make_async_copy(worst_ref, worst_hbm, sems.at[1]),
    )
    for copy in copies:
        copy.start()
    for copy in copies:
        copy.wait()


def body(
    base_real,
    base_reactive,
    voltage,
    rating,
    monitored,
    tile_ids,
    tile_values,
    outage_ids,
    coupling,
    outage_pairs,
):
    blocks = lax.axis_size("blk")
    halves = lax.axis_size("state")
    devices = blocks * halves
    tiles_dev, slots, tile_size, _ = tile_values.shape
    pair_count = outage_pairs.shape[2]
    table_rows = base_real.shape[0] // LANES
    f32 = jnp.float32
    operands = (
        outage_pairs[0],
        coupling[0],
        outage_ids,
        base_real.reshape(table_rows, LANES),
        monitored.reshape(tiles_dev, tile_size),
        base_reactive.reshape(table_rows, LANES),
        voltage.reshape(table_rows, LANES),
        rating.reshape(table_rows, LANES),
        tile_ids,
        tile_values,
    )
    spaces = [pltpu.VMEM] * 8 + [pltpu.SMEM, pltpu.VMEM]
    shapes = (
        jax.ShapeDtypeStruct((tiles_dev, tile_size), f32),
        jax.ShapeDtypeStruct((1, pair_count // halves), f32),
    )
    vmem = pl.BlockSpec(memory_space=pltpu.VMEM)
    results = pl.pallas_call(
        functools.partial(kernel, blocks, halves),
        out_shape=shapes,
        in_specs=[pl.BlockSpec(memory_space=pltpu.HBM)] * 10,
        out_specs=(vmem, vmem),
        scratch_shapes=[space(x.shape, x.dtype) for space, x in zip(spaces, operands)]
        + [
            pltpu.VMEM((8, LANES), jnp.int32),
            pltpu.VMEM((3, table_rows, LANES), f32),
            pltpu.VMEM((3, table_rows, LANES), f32),
            pltpu.VMEM((4, 1, pair_count), f32),
            pltpu.VMEM((4, devices, pair_count), f32),
            pltpu.VMEM((blocks + 1, tile_size, pair_count), jnp.bfloat16),
            pltpu.VMEM((tiles_dev, 3, tile_size, pair_count), f32),
            pltpu.VMEM((LANES, LANES), f32),
            pltpu.VMEM((tiles_dev, tile_size, pair_count), f32),
            pltpu.VMEM((blocks, pair_count), f32),
            pltpu.VMEM((devices, pair_count), f32),
            pltpu.SemaphoreType.DMA((10,)),
            pltpu.SemaphoreType.DMA((2,)),
            pltpu.SemaphoreType.DMA(()),
            pltpu.SemaphoreType.DMA(()),
            pltpu.SemaphoreType.DMA(()),
            pltpu.SemaphoreType.DMA(()),
        ],
        compiler_params=pltpu.CompilerParams(
            collective_id=0, has_side_effects=True, vmem_limit_bytes=48 * 1024 * 1024
        ),
        name="screen",
    )(*[pltpu.with_memory_space_constraint(x, pltpu.HBM) for x in operands])
    hbm = pl.BlockSpec(memory_space=pltpu.HBM)
    peak, worst = pl.pallas_call(
        write_out,
        out_shape=shapes,
        in_specs=[vmem, vmem],
        out_specs=(hbm, hbm),
        scratch_shapes=[pltpu.SemaphoreType.DMA((2,))],
        compiler_params=pltpu.CompilerParams(vmem_limit_bytes=2 * 1024 * 1024),
        name="write_out",
    )(*results)
    return peak.reshape(-1), worst


def solution(mesh):
    every = P(("cases", "blk", "state"))
    by_block = P(("cases", "blk"))
    return jax.shard_map(
        body,
        mesh=mesh,
        in_specs=(every,) * 7 + (by_block,) * 3,
        out_specs=(every, P(("cases", "blk"), "state")),
        check_vma=False,
    )
```

```python
import functools

import jax
import jax.numpy as jnp
from jax import lax
from jax.experimental import pallas as pl
from jax.experimental.pallas import tpu as pltpu
from jax.sharding import PartitionSpec as P

MESH = pl.DeviceIdType.MESH
LANES = 128


def take_lanes(row, lanes):
    spread = jnp.broadcast_to(row, lanes.shape)
    return jnp.take_along_axis(spread, lanes, axis=1, mode="promise_in_bounds")


def lookup(table, high, low, first_row):
    found = jnp.zeros(low.shape, table.dtype)
    for r in range(table.shape[0]):
        found = jnp.where(high == first_row + r, take_lanes(table[r : r + 1], low), found)
    return found


def kernel(
    blocks,
    halves,
    pairs_hbm,
    coup_hbm,
    out_ids_hbm,
    real_hbm,
    mon_hbm,
    react_hbm,
    volt_hbm,
    rating_hbm,
    ids_hbm,
    tiles_hbm,
    peak_ref,
    worst_ref,
    pairs_ref,
    coup_ref,
    out_ids_ref,
    real_ref,
    mon_ref,
    react_ref,
    volt_ref,
    rating_ref,
    ids_ref,
    tiles,
    index,
    table_out,
    table_in,
    pair_out,
    pair_in,
    weights,
    columns,
    rows,
    squares,
    worst_out,
    worst_in,
    load_sems,
    table_sems,
    pair_send,
    pair_recv,
    worst_send,
    worst_recv,
):
    devices = blocks * halves
    tiles_dev, slots, tile_size, _ = tiles_hbm.shape
    table_rows = real_ref.shape[0]
    blk = lax.axis_index("blk")
    state = lax.axis_index("state")
    me = state * blocks + blk

    def each_peer(step):
        if devices <= 16 and blocks & (blocks - 1) == 0:
            turns = [2**j * (1 - 2 * ((blk // 2**j) % 2)) for j in range(blocks.bit_length() - 1)]
            for apart in reversed(range(blocks)):
                to = blk + sum(turn for j, turn in enumerate(turns) if apart >> j & 1)
                step(to, 1 - state)
                if apart:
                    step(to, state)
            return
        step(blk, 1 - state)

        def one_block(i, carry):
            turned = blk + i
            to = jnp.where(turned >= blocks, turned - blocks, turned)
            step(to, state)
            step(to, 1 - state)
            return carry

        lax.fori_loop(1, blocks, one_block, 0)

    loads = [
        pltpu.make_async_copy(source, target, load_sems.at[i])
        for i, (source, target) in enumerate(
            (
                (pairs_hbm, pairs_ref),
                (coup_hbm, coup_ref),
                (out_ids_hbm, out_ids_ref),
                (real_hbm, real_ref),
                (mon_hbm, mon_ref),
                (react_hbm, react_ref),
                (volt_hbm, volt_ref),
                (rating_hbm, rating_ref),
                (ids_hbm, ids_ref),
                (tiles_hbm, tiles),
            )
        )
    ]
    for load in loads[:5]:
        load.start()
    barrier = pltpu.get_barrier_semaphore()

    def greet(to, half):
        there = {"blk": to, "state": half}
        pl.semaphore_signal(barrier, inc=1, device_id=there, device_id_type=MESH)

    each_peer(greet)
    for load in loads[5:]:
        load.start()
    for load in loads[:5]:
        load.wait()

    first, second = pairs_ref[0:1], pairs_ref[1:2]
    spot = lax.broadcasted_iota(jnp.int32, (tile_size, first.shape[1]), 0)
    at_first, at_second = spot == first, spot == second
    one, zero = jnp.float32(1.0), jnp.float32(0.0)
    picks = jnp.concatenate([jnp.where(at_second, one, zero), jnp.where(at_first, one, zero)], axis=1)
    picked = jnp.dot(coup_ref[...], picks.astype(jnp.bfloat16), preferred_element_type=jnp.float32)
    pair_count = first.shape[1]
    s_first_second = jnp.sum(jnp.where(at_first, picked[:, :pair_count], 0.0), axis=0, keepdims=True)
    s_second_first = jnp.sum(jnp.where(at_second, picked[:, pair_count:], 0.0), axis=0, keepdims=True)

    index[...] = jnp.zeros_like(index)
    index[0:tiles_dev] = mon_ref[...]
    out_ids = out_ids_ref[...]
    wide = (8, LANES)
    index[tiles_dev : tiles_dev + 1] = take_lanes(out_ids, jnp.broadcast_to(first, wide))[0:1]
    index[tiles_dev + 1 : tiles_dev + 2] = take_lanes(out_ids, jnp.broadcast_to(second, wide))[0:1]
    high, low = index[...] >> 7, index[...] & (LANES - 1)

    own_row = state * table_rows
    real_own = lookup(real_ref[...], high, low, own_row)
    flows = real_own[tiles_dev : tiles_dev + 2].astype(jnp.bfloat16).astype(jnp.float32)
    is_first = state == 0
    determinant = 1.0 - s_first_second * s_second_first
    pair_out[0] = (flows[0:1] + s_first_second * flows[1:2]) / determinant
    pair_out[1] = (flows[1:2] + s_second_first * flows[0:1]) / determinant
    pair_out[2] = jnp.where(is_first, first, second).astype(jnp.float32)

    pl.semaphore_wait(barrier, devices - 1)

    def send_pairs(to, half):
        pltpu.make_async_remote_copy(
            src_ref=pair_out,
            dst_ref=pair_in.at[:, pl.ds(me, 1)],
            send_sem=pair_send,
            recv_sem=pair_recv,
            device_id={"blk": to, "state": half},
            device_id_type=MESH,
        ).start()

    table_copy = pltpu.make_async_remote_copy(
        src_ref=table_out,
        dst_ref=table_in,
        send_sem=table_sems.at[0],
        recv_sem=table_sems.at[1],
        device_id={"state": 1 - state},
        device_id_type=MESH,
    )
    each_peer(send_pairs)
    for load in loads[5:8]:
        load.wait()
    limit_own = volt_ref[...] * rating_ref[...]
    table_out[0] = real_ref[...]
    table_out[1] = react_ref[...]
    table_out[2] = limit_own
    table_copy.start()
    pair_in[:, pl.ds(me, 1)] = pair_out[...]

    react_own = lookup(react_ref[...], high, low, own_row)
    limit_mine = lookup(limit_own, high, low, own_row)
    weights[0] = jnp.zeros(weights.shape[1:], weights.dtype)
    table_copy.wait_recv()
    other_row = (1 - state) * table_rows
    mine = (high >= own_row) & (high < own_row + table_rows)
    real = jnp.where(mine, real_own, lookup(table_in[0], high, low, other_row))
    react = jnp.where(mine, react_own, lookup(table_in[1], high, low, other_row))
    limit = jnp.where(mine, limit_mine, lookup(table_in[2], high, low, other_row))
    react_sq = react * react
    rows[0:8] = real
    rows[8:16] = react_sq
    rows[16:24] = 1.0 / (limit * limit)
    rows[24:] = jnp.zeros((rows.shape[0] - 24, LANES), jnp.float32)
    upright = rows[...].T
    for t in range(tiles_dev):
        for q in range(3):
            column = upright[:, 8 * q + t : 8 * q + t + 1]
            columns[t, q] = jnp.broadcast_to(column, (tile_size, pair_count))
    loads[8].wait()
    block_of = lax.broadcasted_iota(jnp.int32, (blocks, pair_count), 0)
    worst = jnp.zeros((blocks, pair_count), jnp.float32)
    for t in range(tiles_dev):
        base = columns[t, 0]
        base_peak = jnp.max((base * base + columns[t, 1]) * columns[t, 2], axis=0, keepdims=True)
        absent = block_of >= 0
        for k in range(slots):
            absent = absent & (block_of != ids_ref[t, k])
        worst = jnp.maximum(worst, jnp.where(absent, base_peak, 0.0))
    loads[9].wait()

    peers = pl.ds(0, devices - 1)
    pltpu.make_async_copy(pair_in.at[:, peers], pair_in.at[:, peers], pair_recv).wait()
    w_first = pair_in[0, 0:blocks] + pair_in[0, blocks:]
    w_second = pair_in[1, 0:blocks] + pair_in[1, blocks:]
    first_all, second_all = pair_in[2, 0:blocks], pair_in[2, blocks:]
    places = spot.astype(jnp.float32).astype(jnp.bfloat16).reshape(tile_size // 16, 16, pair_count)

    packed = (16, pair_count)

    def spread(rows_all, b):
        return jnp.broadcast_to(rows_all[b : b + 1], packed).astype(jnp.bfloat16)[None]

    none = jnp.zeros((1, *packed), jnp.bfloat16)
    for b in range(blocks):
        weights[b + 1] = jnp.where(
            places == spread(first_all, b),
            spread(w_first, b),
            jnp.where(places == spread(second_all, b), spread(w_second, b), none),
        ).reshape(tile_size, pair_count)

    for t in range(tiles_dev):

        def absorb(k, delta, most, worst):
            post = columns[t, 0] + delta
            square = post * post
            ratio = (square + columns[t, 1]) * columns[t, 2]
            top = jnp.max(ratio, axis=0, keepdims=True)
            worst = jnp.where(block_of == ids_ref[t, k], jnp.maximum(worst, top), worst)
            return jnp.maximum(most, square), worst

        def two_slots(i, carried):
            k = 2 * i
            first_w, second_w = weights[ids_ref[t, k] + 1], weights[ids_ref[t, k + 1] + 1]
            blank = jnp.zeros_like(first_w)
            both = jnp.concatenate(
                [
                    jnp.concatenate([first_w, blank], axis=1),
                    jnp.concatenate([blank, second_w], axis=1),
                ],
                axis=0,
            )
            held = jnp.concatenate([tiles[t, k], tiles[t, k + 1]], axis=1)
            delta = jnp.dot(held, both, preferred_element_type=jnp.float32)
            carried = absorb(k, delta[:, :pair_count], *carried)
            return absorb(k + 1, delta[:, pair_count:], *carried)

        def one_slot(k, carried):
            weight = weights[ids_ref[t, k] + 1]
            delta = jnp.dot(tiles[t, k], weight, preferred_element_type=jnp.float32)
            return absorb(k, delta, *carried)

        base = columns[t, 0]
        carried = (base * base, worst)
        if slots <= 4:
            for i in range(slots // 2):
                carried = two_slots(i, carried)
        else:
            carried = lax.fori_loop(0, slots // 2, two_slots, carried)
        if slots % 2:
            carried = one_slot(slots - 1, carried)
        most, worst = carried
        squares[t] = most
    worst_out[...] = worst

    def send_worst(to, half):
        pltpu.make_async_remote_copy(
            src_ref=worst_out.at[pl.ds(to, 1)],
            dst_ref=worst_in.at[pl.ds(me, 1)],
            send_sem=worst_send,
            recv_sem=worst_recv,
            device_id={"blk": to, "state": half},
            device_id_type=MESH,
        ).start()

    each_peer(send_worst)
    worst_in[pl.ds(me, 1)] = worst_out[pl.ds(blk, 1)]
    for t in range(tiles_dev):
        most = jnp.max(squares[t].T, axis=0, keepdims=True)
        peak_ref[t : t + 1] = jnp.sqrt((most + rows[8 + t : 9 + t]) * rows[16 + t : 17 + t])

    table_copy.wait_send()
    pltpu.make_async_copy(pair_in.at[:, peers], pair_in.at[:, peers], pair_send).wait()
    pltpu.make_async_copy(worst_in.at[peers], worst_in.at[peers], worst_send).wait()
    pltpu.make_async_copy(worst_in.at[peers], worst_in.at[peers], worst_recv).wait()
    total = jnp.sqrt(jnp.max(worst_in[...], axis=0, keepdims=True))
    half = pair_count // halves
    worst_ref[...] = jnp.where(is_first, total[:, :half], total[:, half:])


def write_out(peak_ref, worst_ref, peak_hbm, worst_hbm, sems):
    copies = (
        pltpu.make_async_copy(peak_ref, peak_hbm, sems.at[0]),
        pltpu.make_async_copy(worst_ref, worst_hbm, sems.at[1]),
    )
    for copy in copies:
        copy.start()
    for copy in copies:
        copy.wait()


def body(
    base_real,
    base_reactive,
    voltage,
    rating,
    monitored,
    tile_ids,
    tile_values,
    outage_ids,
    coupling,
    outage_pairs,
):
    blocks = lax.axis_size("blk")
    halves = lax.axis_size("state")
    devices = blocks * halves
    tiles_dev, slots, tile_size, _ = tile_values.shape
    pair_count = outage_pairs.shape[2]
    table_rows = base_real.shape[0] // LANES
    f32 = jnp.float32
    operands = (
        outage_pairs[0],
        coupling[0],
        outage_ids,
        base_real.reshape(table_rows, LANES),
        monitored.reshape(tiles_dev, tile_size),
        base_reactive.reshape(table_rows, LANES),
        voltage.reshape(table_rows, LANES),
        rating.reshape(table_rows, LANES),
        tile_ids,
        tile_values,
    )
    spaces = [pltpu.VMEM] * 8 + [pltpu.SMEM, pltpu.VMEM]
    shapes = (
        jax.ShapeDtypeStruct((tiles_dev, tile_size), f32),
        jax.ShapeDtypeStruct((1, pair_count // halves), f32),
    )
    vmem = pl.BlockSpec(memory_space=pltpu.VMEM)
    results = pl.pallas_call(
        functools.partial(kernel, blocks, halves),
        out_shape=shapes,
        in_specs=[pl.BlockSpec(memory_space=pltpu.HBM)] * 10,
        out_specs=(vmem, vmem),
        scratch_shapes=[space(x.shape, x.dtype) for space, x in zip(spaces, operands)]
        + [
            pltpu.VMEM((8, LANES), jnp.int32),
            pltpu.VMEM((3, table_rows, LANES), f32),
            pltpu.VMEM((3, table_rows, LANES), f32),
            pltpu.VMEM((3, 1, pair_count), f32),
            pltpu.VMEM((3, devices, pair_count), f32),
            pltpu.VMEM((blocks + 1, tile_size, pair_count), jnp.bfloat16),
            pltpu.VMEM((tiles_dev, 3, tile_size, pair_count), f32),
            pltpu.VMEM((LANES, LANES), f32),
            pltpu.VMEM((tiles_dev, tile_size, pair_count), f32),
            pltpu.VMEM((blocks, pair_count), f32),
            pltpu.VMEM((devices, pair_count), f32),
            pltpu.SemaphoreType.DMA((10,)),
            pltpu.SemaphoreType.DMA((2,)),
            pltpu.SemaphoreType.DMA(()),
            pltpu.SemaphoreType.DMA(()),
            pltpu.SemaphoreType.DMA(()),
            pltpu.SemaphoreType.DMA(()),
        ],
        compiler_params=pltpu.CompilerParams(
            collective_id=0, has_side_effects=True, vmem_limit_bytes=48 * 1024 * 1024
        ),
        name="screen",
    )(*[pltpu.with_memory_space_constraint(x, pltpu.HBM) for x in operands])
    hbm = pl.BlockSpec(memory_space=pltpu.HBM)
    peak, worst = pl.pallas_call(
        write_out,
        out_shape=shapes,
        in_specs=[vmem, vmem],
        out_specs=(hbm, hbm),
        scratch_shapes=[pltpu.SemaphoreType.DMA((2,))],
        compiler_params=pltpu.CompilerParams(vmem_limit_bytes=2 * 1024 * 1024),
        name="write_out",
    )(*results)
    return peak.reshape(-1), worst


def solution(mesh):
    every = P(("cases", "blk", "state"))
    by_block = P(("cases", "blk"))
    return jax.shard_map(
        body,
        mesh=mesh,
        in_specs=(every,) * 7 + (by_block,) * 3,
        out_specs=(every, P(("cases", "blk"), "state")),
        check_vma=False,
    )
```
